32 devices in a mesh: half: 2 (over core), cls: 16 (over z, y, x).
Axes of the slice: x: 2, y: 2, z: 4, core: 2. Of those that a mesh axis runs over, the one named last changes fastest.
Arguments:
- particles: bfloat16 [2, 1024, 128, 128], P('half', 'cls'), may hold values from -6 to 6
- assign: int32 [2, 1024], P('half', 'cls'), may hold values from 0 to 15, as said below
- rotation: int32 [2, 1024], P('half', 'cls'), may hold values from 0 to 35
- group: int32 [2, 1024], P('half', 'cls'), may hold values from 0 to 255
- ctf: float32 [256, 64], replicated, may hold values from -1 to 1
Outputs:
- class_avg: bfloat16 [2, 16, 128, 128], P('half', 'cls')
- residual: bfloat16 [2, 1024, 128, 128], P('half', 'cls')
- scores: bfloat16 [2, 1024, 36], P('half', 'cls')
- leverage: bfloat16 [2, 1024], P('half', 'cls')
The draws below stay inside these ranges and needn't reach their ends.
Inputs may be any that keep to these rules, and one draw needn't show every extreme that they name: `assign`: among the 64 particles of one device no class appears more than 8 times, and one class appears exactly 8 times among every device's particles.
All inputs are finite; a program needn't handle non-finite values.
Results may differ from the reference program's by a relative error of at most 0.0065.
Values may be sent and summed in bfloat16 or wider, within the bound.
A program may use at most 128 MiB of HBM per device.

```python
import jax
import jax.numpy as jnp
from jax import lax

CYCLES = 64
ANGLES = 128
NROT = 36
GROUPS = 256
P_DEV = 64
K = 16
CAP = 8
PART = 1024
N_CLS = 16


def draw_assign(key, part):
    blocks = 2 * K
    slots = K * CAP
    key_hot, key_score, key_order = jax.random.split(key, 3)
    hottest = jax.random.randint(key_hot, (), 0, K)
    noise = jax.random.randint(key_score, (blocks, slots), 0, 1 << 20)
    slot_ids = jnp.arange(slots, dtype=jnp.int32)
    owner_ids = slot_ids // CAP
    ranked = jnp.where(owner_ids[None, :] == hottest, 0, noise + 1) * slots + slot_ids[None, :]
    ordered = jnp.argsort(ranked, axis=1, stable=True)
    chosen = (ordered[:, :P_DEV] // CAP).astype(jnp.int32)
    order_keys = jax.random.split(key_order, blocks)
    shuffles = jax.vmap(lambda sub: jax.random.permutation(sub, P_DEV))(order_keys)
    mixed = jnp.take_along_axis(chosen, shuffles, axis=1)
    return mixed.reshape(2, P_DEV * K).astype(jnp.int32)


def place_ends(drawn, stream_key, least, largest):
    longest = drawn.shape.index(max(drawn.shape))
    spots = []
    for shift in (0, 1):
        where = [jax.random.randint(jax.random.fold_in(stream_key, axis), (), 0, length) for axis, length in enumerate(drawn.shape)]
        where[longest] = (where[longest] + shift) % drawn.shape[longest]
        spots.append(tuple(where))
    return drawn.at[spots[0]].set(least).at[spots[1]].set(largest)


def level_of(own_key, shape, pieces, low, largest):
    loudness = 1.0
    for position, shards_of in pieces:
        draws = jax.random.uniform(jax.random.fold_in(jax.random.fold_in(own_key, 6), position), (shards_of,), jnp.float32, low / len(pieces), largest / len(pieces))
        loudness = loudness * jnp.repeat(jnp.exp(draws), shape[position] // shards_of).reshape((-1,) + (1,) * (len(shape) - 1 - position))
    return loudness


def scatter_about(stream_key, dims, spread, limit, shards=(), kind=jnp.bfloat16):
    level = level_of(stream_key, dims, shards, -0.22, 0.18) if shards else 1.0
    result = jax.random.normal(stream_key, dims, jnp.float32) * spread * level
    return jnp.minimum(jnp.maximum(result, -limit), limit).astype(kind)


def setup_inputs(seed: int = 0) -> dict:
    keys = jax.random.split(jax.random.key(seed), 6)
    return {
        "particles": scatter_about(keys[0], (2, PART, 2 * CYCLES, ANGLES), 1.0, 6.0, ((0, 2), (1, 16))),
        "assign": draw_assign(jax.random.fold_in(keys[5], 71), 0),
        "rotation": place_ends(jax.random.randint(keys[2], (2, PART), 0, NROT), jax.random.fold_in(keys[2], 1), 0, NROT - 1).astype(jnp.int32),
        "group": place_ends(jax.random.randint(keys[3], (2, PART), 0, GROUPS), jax.random.fold_in(keys[3], 1), 0, GROUPS - 1).astype(jnp.int32),
        "ctf": jnp.clip(jax.random.uniform(keys[4], (GROUPS, CYCLES), jnp.float32, -1.0, 1.0), -1.0, 1.0),
    }


wiener_tau = 1.0

def rotation_table(angles):
    turns = jnp.arange(NROT, dtype=jnp.int32)[:, None, None]
    source = jnp.arange(angles, dtype=jnp.int32)[None, :, None]
    target = jnp.arange(angles, dtype=jnp.int32)[None, None, :]
    offset = turns * angles // NROT
    fraction = (turns * angles % NROT).astype(jnp.float32) / NROT
    primary = (source == (target - offset) % angles).astype(jnp.float32)
    neighbor = (source == (target - offset - 1) % angles).astype(jnp.float32)
    return ((1.0 - fraction) * primary + fraction * neighbor).astype(jnp.bfloat16)

def cycle_weights(ctf, group_ids):
    weights = ctf[group_ids]
    return (weights, jnp.concatenate([weights, weights], axis=1))

def split_blocks(images, classes, turns, groups):
    return (images.reshape(N_CLS, P_DEV, 2 * CYCLES, ANGLES), classes.reshape(N_CLS, P_DEV), turns.reshape(N_CLS, P_DEV), groups.reshape(N_CLS, P_DEV))

def align(images, turns, table):
    return jnp.einsum('prb,pba->pra', images.astype(jnp.float32), table[turns], precision=lax.Precision.HIGHEST)

def half_sums(blocks, ctf, table):

    def step(carry, block):
        images, classes, turns, groups = block
        weights, stacked = cycle_weights(ctf, groups)
        aligned = align(images, turns, table)
        onehot = (classes[:, None] == jnp.arange(K, dtype=jnp.int32)[None, :]).astype(jnp.float32)
        weighted = (stacked[:, :, None] * aligned).reshape(images.shape[0], -1)
        class_sum = carry[0] + jnp.dot(onehot.T, weighted, precision=lax.Precision.HIGHEST)
        weight_sum = carry[1] + jnp.dot(onehot.T, weights * weights, precision=lax.Precision.HIGHEST)
        return ((class_sum, weight_sum), None)
    start = (jnp.zeros((K, 2 * CYCLES * ANGLES), jnp.float32), jnp.zeros((K, CYCLES), jnp.float32))
    (class_sum, weight_sum), _ = lax.scan(step, start, blocks)
    return (class_sum, weight_sum)

def half_outputs(blocks, ctf, table, partner_avg, weight_sum):

    def step(carry, block):
        images, classes, turns, groups = block
        weights, stacked = cycle_weights(ctf, groups)
        aligned = align(images, turns, table)
        refs = partner_avg[classes].astype(jnp.float32)
        predicted = (stacked[:, :, None] * refs).astype(jnp.bfloat16)
        residual = (aligned - predicted.astype(jnp.float32)).astype(jnp.bfloat16)
        cross = jnp.einsum('pra,prb->pab', images.astype(jnp.float32), predicted.astype(jnp.float32), precision=lax.Precision.HIGHEST)
        raw = jnp.einsum('pab,tab->pt', cross, table, precision=lax.Precision.HIGHEST)
        pixels = 2 * CYCLES * ANGLES
        first = jnp.sqrt(lax.optimization_barrier(jnp.mean(jnp.square(images.astype(jnp.float32)), axis=(1, 2))) + 1e-05)
        second = jnp.sqrt(lax.optimization_barrier(jnp.mean(jnp.square(predicted.astype(jnp.float32)), axis=(1, 2))) + 1e-05)
        scores = (raw / (jnp.sqrt(jnp.float32(pixels)) * first * second)[:, None]).astype(jnp.bfloat16)
        leverage = lax.optimization_barrier(jnp.mean(weights * weights / (weight_sum[classes] + wiener_tau), axis=1)).astype(jnp.bfloat16)
        return (carry, (residual, scores, leverage))
    _, outputs = lax.scan(step, jnp.float32(0.0), blocks)
    residual, scores, leverage = outputs
    return (residual.reshape(PART, 2 * CYCLES, ANGLES), scores.reshape(PART, NROT), leverage.reshape(PART))

def reference(particles, assign, rotation, group, ctf):
    table = rotation_table(ANGLES).astype(jnp.float32)
    averages = []
    weight_sums = []
    for which in range(2):
        blocks = split_blocks(particles[which], assign[which], rotation[which], group[which])
        class_sum, weight_sum = half_sums(blocks, ctf, table)
        denom = jnp.concatenate([weight_sum, weight_sum], axis=1)[:, :, None] + wiener_tau
        averages.append((class_sum.reshape(K, 2 * CYCLES, ANGLES) / denom).astype(jnp.bfloat16))
        weight_sums.append(weight_sum)
    residuals = []
    score_list = []
    leverages = []
    for which in range(2):
        blocks = split_blocks(particles[which], assign[which], rotation[which], group[which])
        residual, scores, leverage = half_outputs(blocks, ctf, table, averages[1 - which], weight_sums[which])
        residuals.append(residual)
        score_list.append(scores)
        leverages.append(leverage)
    return (jnp.stack(averages), jnp.stack(residuals), jnp.stack(score_list), jnp.stack(leverages))
```

```python
import functools
import math

import jax
import jax.numpy as jnp
from jax import lax
from jax.experimental import pallas as pl
from jax.experimental.pallas import tpu as pltpu
from jax.sharding import PartitionSpec as P

NROT = 36
TAU = 1.0
STEP = 8
MESH = pl.DeviceIdType.MESH
HIGHEST = lax.Precision.HIGHEST
VMEM_BYTES = 40 * 1024 * 1024


def vmem():
    return pl.BlockSpec(memory_space=pltpu.VMEM)


def smem():
    return pl.BlockSpec(memory_space=pltpu.SMEM)


def mix(turn, angles):
    scaled = turn * angles
    offset = scaled // NROT
    fraction = (scaled - offset * NROT).astype(jnp.float32) / NROT
    first = (1.0 - fraction).astype(jnp.bfloat16).astype(jnp.float32)
    second = fraction.astype(jnp.bfloat16).astype(jnp.float32)
    return offset, first, second


def align(image, turn):
    angles = image.shape[1]
    offset, first, second = mix(turn, angles)
    rolled = pltpu.roll(image, offset, 1)
    return first * rolled + second * pltpu.roll(rolled, 1, 1)


def one_hot(row, size):
    places = lax.broadcasted_iota(jnp.int32, (size, row.shape[1]), 0)
    return (places == row).astype(jnp.float32)


def columns_of(ctf, groups):
    return lax.dot_general(
        ctf,
        one_hot(groups, ctf.shape[0]),
        (((0,), (0,)), ((), ())),
        precision=HIGHEST,
        preferred_element_type=jnp.float32,
    )


def fill_columns(columns_ref, ctf_ref, group_ref):
    columns_ref[...] = jnp.zeros_like(columns_ref)
    columns_ref[:, : group_ref.shape[1]] = columns_of(ctf_ref[...], group_ref[...])


def step_columns(columns_ref, step):
    lanes = columns_ref.shape[1]
    return pltpu.roll(columns_ref[...], lax.rem(lanes - step * STEP, lanes), 1)


def stacked(columns, place, lanes):
    column = columns[:, place : place + 1]
    wide = jnp.broadcast_to(column, (columns.shape[0], lanes))
    return jnp.concatenate([wide, wide], axis=0)


def sums_kernel(assign_ref, turn_ref, group_ref, ctf_ref, images_ref, out_ref, total, columns_ref):
    step = pl.program_id(0)

    @pl.when(step == 0)
    def _():
        total[...] = jnp.zeros_like(total)
        fill_columns(columns_ref, ctf_ref, group_ref)

    columns = step_columns(columns_ref, step)
    for place in range(STEP):
        particle = step * STEP + place
        image = images_ref[place].astype(jnp.float32)
        weight = stacked(columns, place, image.shape[1])
        owner = assign_ref[0, particle]
        total[owner] += weight * align(image, turn_ref[0, particle])

    @pl.when(step == pl.num_programs(0) - 1)
    def _():
        out_ref[...] = total[...].astype(jnp.bfloat16)


def share_kernel(
    count,
    sums_ref,
    assign_ref,
    group_ref,
    ctf_ref,
    average_ref,
    lever_ref,
    partner_ref,
    own_code,
    codes,
    landed,
    average,
    code_send,
    code_recv,
    sum_send,
    sum_recv,
    avg_send,
    avg_recv,
):
    half = lax.axis_index("half")
    me = lax.axis_index("cls")
    other = 1 - half
    particles = assign_ref.shape[1]
    shells = ctf_ref.shape[1]

    barrier = pltpu.get_barrier_semaphore()

    def greet(k, _):
        peer = lax.rem(me + k, count)
        pl.semaphore_signal(barrier, inc=1, device_id=(half, peer), device_id_type=MESH)
        return 0

    def greet_other(k, _):
        peer = lax.rem(me + k, count)
        pl.semaphore_signal(barrier, inc=1, device_id=(other, peer), device_id_type=MESH)
        return 0

    lax.fori_loop(1, count, greet, 0)
    lax.fori_loop(0, count, greet_other, 0)
    own_code[0] = jnp.concatenate([assign_ref[...], group_ref[...]], axis=1).astype(jnp.float32)
    pl.semaphore_wait(barrier, 2 * count - 1)

    def code_copy(source, peer):
        return pltpu.make_async_remote_copy(
            src_ref=own_code.at[0],
            dst_ref=codes.at[source],
            send_sem=code_send.at[peer],
            recv_sem=code_recv.at[source],
            device_id=(half, peer),
            device_id_type=MESH,
        )

    def sum_copy(source, peer):
        return pltpu.make_async_remote_copy(
            src_ref=sums_ref.at[peer],
            dst_ref=landed.at[source],
            send_sem=sum_send.at[peer],
            recv_sem=sum_recv.at[source],
            device_id=(half, peer),
            device_id_type=MESH,
        )

    def avg_copy(source, peer):
        return pltpu.make_async_remote_copy(
            src_ref=average,
            dst_ref=partner_ref.at[source],
            send_sem=avg_send.at[peer],
            recv_sem=avg_recv.at[source],
            device_id=(other, peer),
            device_id_type=MESH,
        )

    def send_code(k, _):
        code_copy(me, lax.rem(me + k, count)).start()
        return 0

    def send_sum(k, _):
        sum_copy(me, lax.rem(me + k, count)).start()
        return 0

    lax.fori_loop(1, count, send_code, 0)
    lax.fori_loop(1, count, send_sum, 0)

    def tally(code):
        owners = one_hot(code[:, :particles].astype(jnp.int32), count)
        kinds = one_hot(code[:, particles:].astype(jnp.int32), ctf_ref.shape[0])
        return lax.dot_general(
            owners.astype(jnp.bfloat16),
            kinds.astype(jnp.bfloat16),
            (((1,), (1,)), ((), ())),
            preferred_element_type=jnp.float32,
        )

    def add_code(k, counts):
        source = lax.rem(me + count - k, count)
        code_copy(source, source).wait_recv()
        return counts + tally(codes[source])

    counts = lax.fori_loop(1, count, add_code, tally(own_code[0]))
    table = ctf_ref[...]
    den = jnp.dot(counts, table * table, precision=HIGHEST, preferred_element_type=jnp.float32)
    weights = columns_of(table, group_ref[...])
    chosen = lax.dot_general(
        den,
        one_hot(assign_ref[...], count),
        (((0,), (0,)), ((), ())),
        precision=HIGHEST,
        preferred_element_type=jnp.float32,
    )
    lever = jnp.sum(weights * weights / (chosen + TAU), axis=0, keepdims=True) / shells
    lever_ref[...] = lever.astype(jnp.bfloat16)
    mine = lax.broadcasted_iota(jnp.int32, den.shape, 0) == me
    row = jnp.sum(jnp.where(mine, den, 0.0), axis=0, keepdims=True)
    diagonal = lax.broadcasted_iota(jnp.int32, (shells, shells), 0) == lax.broadcasted_iota(
        jnp.int32, (shells, shells), 1
    )
    column = jnp.sum(jnp.where(diagonal, row, 0.0), axis=1, keepdims=True) + TAU
    denom = jnp.concatenate([column, column], axis=0)

    def add_sum(k, total):
        source = lax.rem(me + count - k, count)
        sum_copy(source, source).wait_recv()
        return total + landed[source].astype(jnp.float32)

    total = lax.fori_loop(1, count, add_sum, sums_ref[me].astype(jnp.float32))
    average[...] = (total / denom).astype(jnp.bfloat16)

    def send_avg(k, _):
        avg_copy(me, lax.rem(me + k, count)).start()
        return 0

    lax.fori_loop(0, count, send_avg, 0)
    average_ref[...] = average[...]

    def finish_own(k, _):
        peer = lax.rem(me + k, count)
        code_copy(me, peer).wait_send()
        sum_copy(me, peer).wait_send()
        return 0

    def finish_avg(k, _):
        peer = lax.rem(me + k, count)
        avg_copy(peer, peer).wait()
        return 0

    lax.fori_loop(1, count, finish_own, 0)
    lax.fori_loop(0, count, finish_avg, 0)


def compare_kernel(
    assign_ref,
    turn_ref,
    group_ref,
    ctf_ref,
    partner_ref,
    images_ref,
    residual_ref,
    scores_ref,
    columns_ref,
    image_power,
    predicted_power,
    folded,
):
    step = pl.program_id(0)

    @pl.when(step == 0)
    def _():
        fill_columns(columns_ref, ctf_ref, group_ref)

    columns = step_columns(columns_ref, step)
    rows, angles = images_ref.shape[1:]

    def fold(values):
        return jnp.sum(values.reshape(rows // 8, 8, angles), axis=0)

    for place in range(STEP):
        particle = step * STEP + place
        raw_image = images_ref[place]
        image = raw_image.astype(jnp.float32)
        weight = stacked(columns, place, angles)
        owner = assign_ref[0, particle]
        rounded = (weight * partner_ref[owner].astype(jnp.float32)).astype(jnp.bfloat16)
        predicted = rounded.astype(jnp.float32)
        residual_ref[place] = (align(image, turn_ref[0, particle]) - predicted).astype(jnp.bfloat16)
        cross = lax.dot_general(
            raw_image, rounded, (((0,), (0,)), ((), ())), preferred_element_type=jnp.float32
        )
        turned = cross[:8]
        for tile in range(1, angles // 8):
            turned += pltpu.roll(cross[tile * 8 : tile * 8 + 8], angles - tile * 8, 1)
        spot = pl.ds(pl.multiple_of(particle * 8, 8), 8)
        folded[spot, :] = turned
        image_power[spot, :] = fold(image * image)
        predicted_power[spot, :] = fold(predicted * predicted)

    @pl.when(step == pl.num_programs(0) - 1)
    def _():
        number = folded.shape[0] // 8

        def part(ref, k):
            return ref[pl.ds(k, number, stride=8), :]

        corr = part(folded, 0)
        first = part(image_power, 0)
        second = part(predicted_power, 0)
        for k in range(1, 8):
            corr += pltpu.roll(part(folded, k), angles - k, 1)
            first += part(image_power, k)
            second += part(predicted_power, k)
        pixels = rows * angles
        first = jnp.sqrt(jnp.sum(first, axis=1, keepdims=True) / pixels + 1e-05)
        second = jnp.sqrt(jnp.sum(second, axis=1, keepdims=True) / pixels + 1e-05)
        turns = lax.broadcasted_iota(jnp.int32, (angles, angles), 1)
        shifts = lax.broadcasted_iota(jnp.int32, (angles, angles), 0)
        offset, one, two = mix(turns, angles)
        offset = lax.rem(offset, angles)
        table = jnp.where(shifts == offset, one, 0.0) + jnp.where(
            shifts == lax.rem(offset + 1, angles), two, 0.0
        )
        raw = jnp.dot(corr, table, precision=HIGHEST, preferred_element_type=jnp.float32)
        scores = raw / (math.sqrt(pixels) * first * second)
        scores_ref[...] = scores[:, :NROT].astype(jnp.bfloat16)


def body(particles, assign, rotation, group, ctf):
    images = particles[0]
    number, rows, angles = images.shape
    shells = ctf.shape[1]
    count = lax.axis_size("cls")
    steps = number // STEP
    params = pltpu.CompilerParams(vmem_limit_bytes=VMEM_BYTES)
    block = pl.BlockSpec((STEP, rows, angles), lambda i: (i, 0, 0))

    sums = pl.pallas_call(
        sums_kernel,
        grid=(steps,),
        out_shape=jax.ShapeDtypeStruct((count, rows, angles), jnp.bfloat16),
        in_specs=[smem(), smem(), vmem(), vmem(), block],
        out_specs=vmem(),
        scratch_shapes=[
            pltpu.VMEM((count, rows, angles), jnp.float32),
            pltpu.VMEM((shells, 128), jnp.float32),
        ],
        compiler_params=params,
        name="class_sums",
    )(assign, rotation, group, ctf, images)

    average, leverage, partner = pl.pallas_call(
        functools.partial(share_kernel, count),
        out_shape=(
            jax.ShapeDtypeStruct((rows, angles), jnp.bfloat16),
            jax.ShapeDtypeStruct((1, number), jnp.bfloat16),
            jax.ShapeDtypeStruct((count, rows, angles), jnp.bfloat16),
        ),
        in_specs=[vmem(), vmem(), vmem(), vmem()],
        out_specs=(vmem(), vmem(), pl.BlockSpec(memory_space=pl.ANY)),
        scratch_shapes=[
            pltpu.VMEM((1, 1, 2 * number), jnp.float32),
            pltpu.VMEM((count, 1, 2 * number), jnp.float32),
            pltpu.VMEM((count, rows, angles), jnp.bfloat16),
            pltpu.VMEM((rows, angles), jnp.bfloat16),
        ]
        + [pltpu.SemaphoreType.DMA((count,))] * 6,
        compiler_params=pltpu.CompilerParams(
            collective_id=0, has_side_effects=True, vmem_limit_bytes=VMEM_BYTES
        ),
        name="share",
    )(sums, assign, group, ctf)

    residual, scores = pl.pallas_call(
        compare_kernel,
        grid=(steps,),
        out_shape=(
            jax.ShapeDtypeStruct((number, rows, angles), jnp.bfloat16),
            jax.ShapeDtypeStruct((number, NROT), jnp.bfloat16),
        ),
        in_specs=[smem(), smem(), vmem(), vmem(), vmem(), block],
        out_specs=(block, vmem()),
        scratch_shapes=[pltpu.VMEM((shells, 128), jnp.float32)]
        + [pltpu.VMEM((number * 8, angles), jnp.float32)] * 3,
        compiler_params=params,
        name="compare",
    )(assign, rotation, group, ctf, partner, images)
    return (average[None, None], residual[None], scores[None], leverage)


def solution(mesh):
    in_specs = (
        P("half", "cls", None, None),
        P("half", "cls"),
        P("half", "cls"),
        P("half", "cls"),
        P(),
    )
    out_specs = (
        P("half", "cls", None, None),
        P("half", "cls", None, None),
        P("half", "cls", None),
        P("half", "cls"),
    )
    return jax.shard_map(body, mesh=mesh, in_specs=in_specs, out_specs=out_specs, check_vma=False)
```

```python
import functools
import math

import jax
import jax.numpy as jnp
from jax import lax
from jax.experimental import pallas as pl
from jax.experimental.pallas import tpu as pltpu
from jax.sharding import PartitionSpec as P

NROT = 36
TAU = 1.0
STEP = 8
QUAD = 4
MESH = pl.DeviceIdType.MESH
HIGHEST = lax.Precision.HIGHEST
VMEM_BYTES = 24 * 1024 * 1024
WIDE_BYTES = 62 * 1024 * 1024


def vmem():
    return pl.BlockSpec(memory_space=pltpu.VMEM)


def smem():
    return pl.BlockSpec(memory_space=pltpu.SMEM)


def mix(turn, angles):
    scaled = turn * angles
    offset = scaled // NROT
    fraction = (scaled - offset * NROT).astype(jnp.float32) / NROT
    first = (1.0 - fraction).astype(jnp.bfloat16).astype(jnp.float32)
    second = fraction.astype(jnp.bfloat16).astype(jnp.float32)
    return offset, first, second


def align(image, turn):
    angles = image.shape[1]
    offset, first, second = mix(turn, angles)
    rolled = pltpu.roll(image, offset, 1)
    return first * rolled + second * pltpu.roll(rolled, 1, 1)


def one_hot(row, size):
    places = lax.broadcasted_iota(jnp.int32, (size, row.shape[1]), 0)
    return (places == row).astype(jnp.float32)


def columns_of(ctf, groups):
    return lax.dot_general(
        ctf,
        one_hot(groups, ctf.shape[1]),
        (((1,), (0,)), ((), ())),
        precision=HIGHEST,
        preferred_element_type=jnp.float32,
    )


def fill_columns(columns_ref, ctf_ref, group_ref):
    columns_ref[...] = jnp.zeros_like(columns_ref)
    columns_ref[:, : group_ref.shape[1]] = columns_of(ctf_ref[...], group_ref[...])


def step_columns(columns_ref, step):
    lanes = columns_ref.shape[1]
    return pltpu.roll(columns_ref[...], lax.rem(lanes - step * STEP, lanes), 1)


def stacked(columns, place, lanes):
    column = columns[:, place : place + 1]
    wide = jnp.broadcast_to(column, (columns.shape[0], lanes))
    return jnp.concatenate([wide, wide], axis=0)


def sums_kernel(assign_ref, turn_ref, group_ref, ctf_ref, images_ref, out_ref, total, columns_ref):
    step = pl.program_id(0)

    @pl.when(step == 0)
    def _():
        total[...] = jnp.zeros_like(total)
        fill_columns(columns_ref, ctf_ref, group_ref)

    columns = step_columns(columns_ref, step)
    for place in range(STEP):
        particle = step * STEP + place
        image = images_ref[place].astype(jnp.float32)
        weight = stacked(columns, place, image.shape[1])
        owner = assign_ref[0, particle]
        total[owner] += weight * align(image, turn_ref[0, particle])

    @pl.when(step == pl.num_programs(0) - 1)
    def _():
        out_ref[...] = total[...].astype(jnp.bfloat16)


def share_kernel(
    count,
    sums_ref,
    assign_ref,
    group_ref,
    ctf_ref,
    average_ref,
    lever_ref,
    partner_ref,
    own_code,
    codes,
    landed,
    staged,
    gathered,
    average,
    code_send,
    code_recv,
    quad_send,
    quad_recv,
    far_send,
    far_recv,
    avg_send,
    pass_send,
    avg_recv,
):
    half = lax.axis_index("half")
    me = lax.axis_index("cls")
    other = 1 - half
    layers = count // QUAD
    layer = me // QUAD
    spot = me % QUAD
    particles = assign_ref.shape[1]

    barrier = pltpu.get_barrier_semaphore()

    def greet(k, _):
        peer = lax.rem(me + k, count)
        pl.semaphore_signal(barrier, inc=1, device_id=(half, peer), device_id_type=MESH)
        return 0

    def greet_other(k, _):
        peer = lax.rem(layer + k, layers) * QUAD + spot
        pl.semaphore_signal(barrier, inc=1, device_id=(other, peer), device_id_type=MESH)
        return 0

    lax.fori_loop(1, count, greet, 0)
    lax.fori_loop(0, layers, greet_other, 0)
    own_code[0] = jnp.concatenate([assign_ref[...], group_ref[...]], axis=1).astype(jnp.float32)
    pl.semaphore_wait(barrier, count - 1 + layers)

    def code_copy(source, peer):
        return pltpu.make_async_remote_copy(
            src_ref=own_code.at[0],
            dst_ref=codes.at[source],
            send_sem=code_send.at[peer],
            recv_sem=code_recv.at[source],
            device_id=(half, peer),
            device_id_type=MESH,
        )

    def quad_copy(level, source, target):
        return pltpu.make_async_remote_copy(
            src_ref=sums_ref.at[level * QUAD + target],
            dst_ref=landed.at[level * QUAD + source],
            send_sem=quad_send.at[level * QUAD + target],
            recv_sem=quad_recv.at[level * QUAD + source],
            device_id=(half, layer * QUAD + target),
            device_id_type=MESH,
        )

    def far_copy(source, target):
        return pltpu.make_async_remote_copy(
            src_ref=staged.at[target],
            dst_ref=gathered.at[source],
            send_sem=far_send.at[target],
            recv_sem=far_recv.at[source],
            device_id=(half, target * QUAD + spot),
            device_id_type=MESH,
        )

    def avg_copy(source, target):
        return pltpu.make_async_remote_copy(
            src_ref=average,
            dst_ref=partner_ref.at[source * QUAD + spot],
            send_sem=avg_send.at[target],
            recv_sem=avg_recv.at[source * QUAD + spot],
            device_id=(other, target * QUAD + spot),
            device_id_type=MESH,
        )

    def pass_copy(level, source, target):
        return pltpu.make_async_remote_copy(
            src_ref=partner_ref.at[level * QUAD + source],
            dst_ref=partner_ref.at[level * QUAD + source],
            send_sem=pass_send.at[level * QUAD + target],
            recv_sem=avg_recv.at[level * QUAD + source],
            device_id=(half, layer * QUAD + target),
            device_id_type=MESH,
        )

    def send_code(k, _):
        code_copy(me, lax.rem(me + k, count)).start()
        return 0

    def send_quad(k, _):
        level = lax.rem(layer + k, layers)
        for j in range(1, QUAD):
            quad_copy(level, spot, lax.rem(spot + j, QUAD)).start()
        return 0

    lax.fori_loop(1, layers + 1, send_quad, 0)
    lax.fori_loop(1, count, send_code, 0)

    def quad_sum(level):
        total = sums_ref[level * QUAD + spot].astype(jnp.float32)
        for j in range(1, QUAD):
            source = lax.rem(spot + j, QUAD)
            quad_copy(level, source, source).wait_recv()
            total += landed[level * QUAD + source].astype(jnp.float32)
        return total

    def send_far(k, _):
        level = lax.rem(layer + k, layers)
        staged[level] = quad_sum(level).astype(jnp.bfloat16)
        far_copy(layer, level).start()
        return 0

    lax.fori_loop(1, layers, send_far, 0)

    def tally(code):
        owners = one_hot(code[:, :particles].astype(jnp.int32), count)
        kinds = one_hot(code[:, particles:].astype(jnp.int32), ctf_ref.shape[1])
        return lax.dot_general(
            owners.astype(jnp.bfloat16),
            kinds.astype(jnp.bfloat16),
            (((1,), (1,)), ((), ())),
            preferred_element_type=jnp.float32,
        )

    def add_code(k, counts):
        source = lax.rem(me + count - k, count)
        code_copy(source, source).wait_recv()
        return counts + tally(codes[source])

    counts = lax.fori_loop(1, count, add_code, tally(own_code[0]))
    table = ctf_ref[...]
    den = lax.dot_general(
        table * table,
        counts,
        (((1,), (1,)), ((), ())),
        precision=HIGHEST,
        preferred_element_type=jnp.float32,
    )
    mine = lax.broadcasted_iota(jnp.int32, den.shape, 1) == me
    column = jnp.sum(jnp.where(mine, den, 0.0), axis=1, keepdims=True) + TAU
    denom = jnp.concatenate([column, column], axis=0)

    def add_far(k, total):
        source = lax.rem(layer + count - k, layers)
        far_copy(source, source).wait_recv()
        return total + gathered[source].astype(jnp.float32)

    total = lax.fori_loop(1, layers, add_far, quad_sum(layer))
    average[...] = (total / denom).astype(jnp.bfloat16)

    def send_avg(k, _):
        avg_copy(layer, lax.rem(layer + k, layers)).start()
        return 0

    lax.fori_loop(0, layers, send_avg, 0)
    average_ref[...] = average[...]
    weights = columns_of(table, group_ref[...])
    chosen = jnp.dot(
        den,
        one_hot(assign_ref[...], count),
        precision=HIGHEST,
        preferred_element_type=jnp.float32,
    )
    lever = jnp.sum(weights * weights / (chosen + TAU), axis=0, keepdims=True)
    lever_ref[...] = (lever / table.shape[0]).astype(jnp.bfloat16)

    def pass_on(k, _):
        level = lax.rem(layer + k, layers)
        avg_copy(level, level).wait_recv()
        for j in range(1, QUAD):
            pass_copy(level, spot, lax.rem(spot + j, QUAD)).start()
        return 0

    lax.fori_loop(0, layers, pass_on, 0)

    def finish_code(k, _):
        code_copy(me, lax.rem(me + k, count)).wait_send()
        return 0

    def finish_far(k, _):
        far_copy(layer, lax.rem(layer + k, layers)).wait_send()
        return 0

    def finish_level(k, _):
        level = lax.rem(layer + k, layers)
        avg_copy(layer, level).wait_send()
        for j in range(1, QUAD):
            peer = lax.rem(spot + j, QUAD)
            quad_copy(level, spot, peer).wait_send()
            pass_copy(level, peer, peer).wait_recv()
            pass_copy(level, spot, peer).wait_send()
        return 0

    lax.fori_loop(1, count, finish_code, 0)
    lax.fori_loop(1, layers, finish_far, 0)
    lax.fori_loop(0, layers, finish_level, 0)


def compare_kernel(
    assign_ref,
    turn_ref,
    group_ref,
    ctf_ref,
    partner_ref,
    average_ref,
    lever_ref,
    images_ref,
    residual_ref,
    scores_ref,
    average_out,
    lever_out,
    columns_ref,
    image_power,
    predicted_power,
    folded,
):
    step = pl.program_id(0)

    @pl.when(step == 0)
    def _():
        fill_columns(columns_ref, ctf_ref, group_ref)
        average_out[...] = average_ref[...]
        lever_out[...] = lever_ref[...]

    columns = step_columns(columns_ref, step)
    rows, angles = images_ref.shape[1:]

    def fold(values):
        return jnp.sum(values.reshape(rows // 8, 8, angles), axis=0)

    for place in range(STEP):
        particle = step * STEP + place
        raw_image = images_ref[place]
        image = raw_image.astype(jnp.float32)
        weight = stacked(columns, place, angles)
        owner = assign_ref[0, particle]
        rounded = (weight * partner_ref[owner].astype(jnp.float32)).astype(jnp.bfloat16)
        predicted = rounded.astype(jnp.float32)
        residual_ref[place] = (align(image, turn_ref[0, particle]) - predicted).astype(jnp.bfloat16)
        cross = lax.dot_general(
            raw_image, rounded, (((0,), (0,)), ((), ())), preferred_element_type=jnp.float32
        )
        turned = cross[:8]
        for tile in range(1, angles // 8):
            turned += pltpu.roll(cross[tile * 8 : tile * 8 + 8], angles - tile * 8, 1)
        spot = pl.ds(pl.multiple_of(particle * 8, 8), 8)
        folded[spot, :] = turned
        image_power[spot, :] = fold(image * image)
        predicted_power[spot, :] = fold(predicted * predicted)

    @pl.when(step == pl.num_programs(0) - 1)
    def _():
        number = folded.shape[0] // 8

        def part(ref, k):
            return ref[pl.ds(k, number, stride=8), :]

        corr = part(folded, 0)
        first = part(image_power, 0)
        second = part(predicted_power, 0)
        for k in range(1, 8):
            corr += pltpu.roll(part(folded, k), angles - k, 1)
            first += part(image_power, k)
            second += part(predicted_power, k)
        pixels = rows * angles
        ones = jnp.ones((1, angles), jnp.float32)

        def across(left, right, dims):
            return lax.dot_general(
                left, right, (dims, ((), ())), precision=HIGHEST, preferred_element_type=jnp.float32
            )

        first = jnp.sqrt(across(ones, first, ((1,), (1,))) / pixels + 1e-05)
        second = jnp.sqrt(across(ones, second, ((1,), (1,))) / pixels + 1e-05)
        turns = lax.broadcasted_iota(jnp.int32, (angles, angles), 1)
        shifts = lax.broadcasted_iota(jnp.int32, (angles, angles), 0)
        offset, one, two = mix(turns, angles)
        offset = lax.rem(offset, angles)
        table = jnp.where(shifts == offset, one, 0.0) + jnp.where(
            shifts == lax.rem(offset + 1, angles), two, 0.0
        )
        raw = across(table, corr, ((0,), (1,)))
        scores = raw / (math.sqrt(pixels) * first * second)
        scores_ref[...] = scores[:NROT].astype(jnp.bfloat16)


def body(particles, assign, rotation, group, ctf):
    images = particles[0]
    number, rows, angles = images.shape
    table = ctf.T
    shells = ctf.shape[1]
    count = lax.axis_size("cls")
    layers = count // QUAD
    steps = number // STEP
    params = pltpu.CompilerParams(vmem_limit_bytes=VMEM_BYTES)
    block = pl.BlockSpec((STEP, rows, angles), lambda i: (i, 0, 0))

    sums = pl.pallas_call(
        sums_kernel,
        grid=(steps,),
        out_shape=jax.ShapeDtypeStruct((count, rows, angles), jnp.bfloat16),
        in_specs=[smem(), smem(), vmem(), vmem(), block],
        out_specs=vmem(),
        scratch_shapes=[
            pltpu.VMEM((count, rows, angles), jnp.float32),
            pltpu.VMEM((shells, 128), jnp.float32),
        ],
        compiler_params=pltpu.CompilerParams(vmem_limit_bytes=WIDE_BYTES),
        name="class_sums",
    )(assign, rotation, group, table, images)

    average, lever, partner = pl.pallas_call(
        functools.partial(share_kernel, count),
        out_shape=(
            jax.ShapeDtypeStruct((rows, angles), jnp.bfloat16),
            jax.ShapeDtypeStruct((1, number), jnp.bfloat16),
            jax.ShapeDtypeStruct((count, rows, angles), jnp.bfloat16),
        ),
        in_specs=[vmem(), vmem(), vmem(), vmem()],
        out_specs=(vmem(), vmem(), pl.BlockSpec(memory_space=pl.ANY)),
        scratch_shapes=[
            pltpu.VMEM((1, 1, 2 * number), jnp.float32),
            pltpu.VMEM((count, 1, 2 * number), jnp.float32),
            pltpu.VMEM((count, rows, angles), jnp.bfloat16),
            pltpu.VMEM((layers, rows, angles), jnp.bfloat16),
            pltpu.VMEM((layers, rows, angles), jnp.bfloat16),
            pltpu.VMEM((rows, angles), jnp.bfloat16),
        ]
        + [pltpu.SemaphoreType.DMA((count,))] * 4
        + [pltpu.SemaphoreType.DMA((layers,))] * 3
        + [pltpu.SemaphoreType.DMA((count,))] * 2,
        compiler_params=pltpu.CompilerParams(
            collective_id=0, has_side_effects=True, vmem_limit_bytes=VMEM_BYTES
        ),
        name="share",
    )(sums, assign, group, table)

    residual, scores, average, lever = pl.pallas_call(
        compare_kernel,
        grid=(steps,),
        out_shape=(
            jax.ShapeDtypeStruct((number, rows, angles), jnp.bfloat16),
            jax.ShapeDtypeStruct((NROT, number), jnp.bfloat16),
            jax.ShapeDtypeStruct((rows, angles), jnp.bfloat16),
            jax.ShapeDtypeStruct((1, number), jnp.bfloat16),
        ),
        in_specs=[smem(), smem()] + [vmem()] * 5 + [block],
        out_specs=(block, vmem(), vmem(), vmem()),
        scratch_shapes=[pltpu.VMEM((shells, 128), jnp.float32)]
        + [pltpu.VMEM((number * 8, angles), jnp.float32)] * 3,
        compiler_params=params,
        name="compare",
    )(assign, rotation, group, table, partner, average, lever, images)
    return (average[None, None], residual[None], scores.T[None], lever)


def solution(mesh):
    in_specs = (
        P("half", "cls", None, None),
        P("half", "cls"),
        P("half", "cls"),
        P("half", "cls"),
        P(),
    )
    out_specs = (
        P("half", "cls", None, None),
        P("half", "cls", None, None),
        P("half", "cls", None),
        P("half", "cls"),
    )
    return jax.shard_map(body, mesh=mesh, in_specs=in_specs, out_specs=out_specs, check_vma=False)
```

```python
import functools
import math

import jax
import jax.numpy as jnp
from jax import lax
from jax.experimental import pallas as pl
from jax.experimental.pallas import tpu as pltpu
from jax.sharding import PartitionSpec as P

NROT = 36
TAU = 1.0
STEP = 8
QUAD = 4
MESH = pl.DeviceIdType.MESH
HIGHEST = lax.Precision.HIGHEST
WIDE_BYTES = 62 * 1024 * 1024


def vmem():
    return pl.BlockSpec(memory_space=pltpu.VMEM)


def anywhere():
    return pl.BlockSpec(memory_space=pl.ANY)


def mix(turn, angles):
    scaled = turn * angles
    offset = scaled // NROT
    fraction = (scaled - offset * NROT).astype(jnp.float32) / NROT
    first = (1.0 - fraction).astype(jnp.bfloat16).astype(jnp.float32)
    second = fraction.astype(jnp.bfloat16).astype(jnp.float32)
    return offset, first, second


def align(image, turn):
    angles = image.shape[1]
    offset, first, second = mix(turn, angles)
    rolled = pltpu.roll(image, offset, 1)
    return first * rolled.astype(jnp.float32) + second * pltpu.roll(rolled, 1, 1).astype(
        jnp.float32
    )


def one_hot(row, size):
    places = lax.broadcasted_iota(jnp.int32, (size, row.shape[1]), 0)
    return (places == row).astype(jnp.float32)


def columns_of(ctf, groups):
    return lax.dot_general(
        ctf,
        one_hot(groups, ctf.shape[1]),
        (((1,), (0,)), ((), ())),
        precision=HIGHEST,
        preferred_element_type=jnp.float32,
    )


def fill_columns(columns_ref, ctf_ref, group_ref):
    columns_ref[...] = jnp.zeros_like(columns_ref)
    columns_ref[:, : group_ref.shape[1]] = columns_of(ctf_ref[...], group_ref[...])


def step_columns(columns_ref, step):
    lanes = columns_ref.shape[1]
    return pltpu.roll(columns_ref[...], lax.rem(lanes - step * STEP, lanes), 1)


def stacked(columns, place, lanes):
    column = columns[:, place : place + 1]
    wide = jnp.broadcast_to(column, (columns.shape[0], lanes))
    return jnp.concatenate([wide, wide], axis=0)


def share_kernel(
    count,
    cap,
    images_hbm,
    assign_hbm,
    turn_hbm,
    group_hbm,
    ctf_hbm,
    average_ref,
    lever_ref,
    partner_ref,
    images_ref,
    assign_ref,
    turn_ref,
    group_ref,
    ctf_ref,
    order_row,
    order_ref,
    slot_weights,
    sums_ref,
    own_sums,
    own_code,
    codes,
    landed,
    staged,
    gathered,
    average,
    loads,
    code_send,
    code_recv,
    quad_send,
    quad_recv,
    far_send,
    far_recv,
    avg_send,
    pass_send,
    avg_recv,
):
    half = lax.axis_index("half")
    me = lax.axis_index("cls")
    other = 1 - half
    layers = count // QUAD
    layer = me // QUAD
    spot = me % QUAD
    particles = assign_ref.shape[1]
    slots = count * cap

    pairs = (
        (assign_hbm, assign_ref),
        (group_hbm, group_ref),
        (ctf_hbm, ctf_ref),
        (turn_hbm, turn_ref),
        (images_hbm, images_ref),
    )
    moves = [pltpu.make_async_copy(a, b, loads.at[n]) for n, (a, b) in enumerate(pairs)]
    for move in moves:
        move.start()

    barrier = pltpu.get_barrier_semaphore()

    def greet(k, _):
        peer = lax.rem(me + k, count)
        pl.semaphore_signal(barrier, inc=1, device_id=(half, peer), device_id_type=MESH)
        return 0

    def greet_other(k, _):
        peer = lax.rem(layer + k, layers) * QUAD + spot
        pl.semaphore_signal(barrier, inc=1, device_id=(other, peer), device_id_type=MESH)
        return 0

    lax.fori_loop(1, count, greet, 0)
    lax.fori_loop(0, layers, greet_other, 0)
    for move in moves[:3]:
        move.wait()
    own_code[0] = jnp.concatenate([assign_ref[...], group_ref[...]], axis=1).astype(jnp.float32)
    line = lax.broadcasted_iota(jnp.int32, (particles, particles), 0)
    across = lax.broadcasted_iota(jnp.int32, (particles, particles), 1)

    def as_column(row):
        return jnp.sum(jnp.where(line == across, row, 0), axis=1, keepdims=True)

    same = (as_column(assign_ref[...]) == assign_ref[...]) & (line < across)
    rank = jnp.sum(jnp.where(same, 1, 0), axis=0, keepdims=True)
    places = assign_ref[...] * cap + rank
    taken = one_hot(places, slots)
    filled = as_column(places) == lax.broadcasted_iota(jnp.int32, (particles, slots), 1)
    numbers = lax.broadcasted_iota(jnp.int32, (particles, slots), 0)
    order_row[...] = jnp.sum(jnp.where(filled, numbers, 0), axis=0, keepdims=True)

    def to_slots(values):
        return lax.dot_general(
            values,
            taken,
            (((1,), (1,)), ((), ())),
            precision=HIGHEST,
            preferred_element_type=jnp.float32,
        )

    order_move = pltpu.make_async_copy(order_row, order_ref, loads.at[0])
    order_move.start()
    weights = columns_of(ctf_ref[...], group_ref[...])
    slot_weights[...] = to_slots(weights)
    order_move.wait()
    for move in moves[3:]:
        move.wait()
    pl.semaphore_wait(barrier, count - 1 + layers)

    def code_copy(source, peer):
        return pltpu.make_async_remote_copy(
            src_ref=own_code.at[0],
            dst_ref=codes.at[source],
            send_sem=code_send.at[peer],
            recv_sem=code_recv.at[source],
            device_id=(half, peer),
            device_id_type=MESH,
        )

    def quad_copy(level, source, target):
        return pltpu.make_async_remote_copy(
            src_ref=sums_ref.at[level * QUAD + target],
            dst_ref=landed.at[level * QUAD + source],
            send_sem=quad_send.at[level * QUAD + target],
            recv_sem=quad_recv.at[level * QUAD + source],
            device_id=(half, layer * QUAD + target),
            device_id_type=MESH,
        )

    def far_copy(source, target):
        return pltpu.make_async_remote_copy(
            src_ref=staged.at[target],
            dst_ref=gathered.at[source],
            send_sem=far_send.at[target],
            recv_sem=far_recv.at[source],
            device_id=(half, target * QUAD + spot),
            device_id_type=MESH,
        )

    def avg_copy(source, target):
        return pltpu.make_async_remote_copy(
            src_ref=average,
            dst_ref=partner_ref.at[source * QUAD + spot],
            send_sem=avg_send.at[target],
            recv_sem=avg_recv.at[source * QUAD + spot],
            device_id=(other, target * QUAD + spot),
            device_id_type=MESH,
        )

    def pass_copy(level, source, target):
        return pltpu.make_async_remote_copy(
            src_ref=partner_ref.at[level * QUAD + source],
            dst_ref=partner_ref.at[level * QUAD + source],
            send_sem=pass_send.at[level * QUAD + target],
            recv_sem=avg_recv.at[level * QUAD + source],
            device_id=(half, layer * QUAD + target),
            device_id_type=MESH,
        )

    def send_code(k, _):
        code_copy(me, lax.rem(me + k, count)).start()
        return 0

    lax.fori_loop(1, count, send_code, 0)

    def class_sum(owner):
        columns = pltpu.roll(slot_weights[...], lax.rem(slots - owner * cap, slots), 1)
        total = jnp.zeros(images_ref.shape[1:], jnp.float32)
        for place in range(cap):
            particle = jnp.clip(order_ref[0, owner * cap + place], 0, images_ref.shape[0] - 1)
            image = align(images_ref[particle], turn_ref[0, particle])
            total += stacked(columns, place, image.shape[1]) * image
        return total

    def quad_sum(level):
        total = own_sums[level]
        for j in range(1, QUAD):
            source = lax.rem(spot + j, QUAD)
            quad_copy(level, source, source).wait_recv()
            total += landed[level * QUAD + source].astype(jnp.float32)
        return total

    def send_far(k, _):
        level = lax.rem(layer + k, layers)
        staged[level] = quad_sum(level).astype(jnp.bfloat16)
        far_copy(layer, level).start()
        return 0

    def sum_level(k, _):
        level = lax.rem(layer + k, layers)
        for j in range(1, QUAD):
            target = lax.rem(spot + j, QUAD)
            sums_ref[level * QUAD + target] = class_sum(level * QUAD + target).astype(jnp.bfloat16)
            quad_copy(level, spot, target).start()
        own_sums[level] = class_sum(level * QUAD + spot)

        @pl.when(k > 1)
        def _():
            send_far(k - 1, 0)

        return 0

    lax.fori_loop(1, layers + 1, sum_level, 0)

    def tally(code):
        owners = one_hot(code[:, :particles].astype(jnp.int32), count)
        kinds = one_hot(code[:, particles:].astype(jnp.int32), ctf_ref.shape[1])
        return lax.dot_general(
            owners.astype(jnp.bfloat16),
            kinds.astype(jnp.bfloat16),
            (((1,), (1,)), ((), ())),
            preferred_element_type=jnp.float32,
        )

    def add_code(k, counts):
        source = lax.rem(me + count - k, count)
        code_copy(source, source).wait_recv()
        return counts + tally(codes[source])

    counts = lax.fori_loop(1, count, add_code, tally(own_code[0]))
    table = ctf_ref[...]
    den = lax.dot_general(
        table * table,
        counts,
        (((1,), (1,)), ((), ())),
        precision=HIGHEST,
        preferred_element_type=jnp.float32,
    )
    mine = lax.broadcasted_iota(jnp.int32, den.shape, 1) == me
    column = jnp.sum(jnp.where(mine, den, 0.0), axis=1, keepdims=True) + TAU
    denom = jnp.concatenate([column, column], axis=0)

    def add_far(k, total):
        source = lax.rem(layer + count - k, layers)
        far_copy(source, source).wait_recv()
        return total + gathered[source].astype(jnp.float32)

    total = lax.fori_loop(1, layers, add_far, quad_sum(layer))
    average[...] = (total / denom).astype(jnp.bfloat16)

    def send_avg(k, _):
        avg_copy(layer, lax.rem(layer + k, layers)).start()
        return 0

    lax.fori_loop(0, layers, send_avg, 0)
    average_ref[...] = average[...]
    chosen = jnp.dot(
        den,
        one_hot(assign_ref[...], count),
        precision=HIGHEST,
        preferred_element_type=jnp.float32,
    )
    lever = jnp.sum(weights * weights / (chosen + TAU), axis=0, keepdims=True)
    lever_ref[...] = (lever / table.shape[0]).astype(jnp.bfloat16)

    def pass_on(k, _):
        level = lax.rem(layer + k, layers)
        avg_copy(level, level).wait_recv()
        for j in range(1, QUAD):
            pass_copy(level, spot, lax.rem(spot + j, QUAD)).start()
        return 0

    lax.fori_loop(0, layers, pass_on, 0)

    def finish_code(k, _):
        code_copy(me, lax.rem(me + k, count)).wait_send()
        return 0

    def finish_far(k, _):
        far_copy(layer, lax.rem(layer + k, layers)).wait_send()
        return 0

    def finish_level(k, _):
        level = lax.rem(layer + k, layers)
        avg_copy(layer, level).wait_send()
        for j in range(1, QUAD):
            peer = lax.rem(spot + j, QUAD)
            quad_copy(level, spot, peer).wait_send()
            pass_copy(level, peer, peer).wait_recv()
            pass_copy(level, spot, peer).wait_send()
        return 0

    lax.fori_loop(1, count, finish_code, 0)
    lax.fori_loop(1, layers, finish_far, 0)
    lax.fori_loop(0, layers, finish_level, 0)


def compare_kernel(
    assign_hbm,
    turn_hbm,
    group_hbm,
    ctf_hbm,
    partner_hbm,
    average_hbm,
    lever_hbm,
    images_ref,
    residual_ref,
    scores_ref,
    average_out,
    lever_out,
    assign_ref,
    turn_ref,
    group_ref,
    ctf_ref,
    partner_ref,
    loads,
    columns_ref,
    image_power,
    predicted_power,
    folded,
):
    step = pl.program_id(0)

    @pl.when(step == 0)
    def _():
        pairs = (
            (group_hbm, group_ref),
            (ctf_hbm, ctf_ref),
            (assign_hbm, assign_ref),
            (turn_hbm, turn_ref),
            (average_hbm, average_out),
            (lever_hbm, lever_out),
            (partner_hbm, partner_ref),
        )
        moves = [pltpu.make_async_copy(a, b, loads.at[n]) for n, (a, b) in enumerate(pairs)]
        for move in moves:
            move.start()
        for move in moves[:2]:
            move.wait()
        fill_columns(columns_ref, ctf_ref, group_ref)
        for move in moves[2:]:
            move.wait()

    columns = step_columns(columns_ref, step)
    rows, angles = images_ref.shape[1:]

    def fold(values):
        return jnp.sum(values.reshape(rows // 8, 8, angles), axis=0)

    for place in range(STEP):
        particle = step * STEP + place
        raw_image = images_ref[place]
        image = raw_image.astype(jnp.float32)
        weight = stacked(columns, place, angles)
        owner = assign_ref[0, particle]
        rounded = (weight * partner_ref[owner].astype(jnp.float32)).astype(jnp.bfloat16)
        predicted = rounded.astype(jnp.float32)
        residual_ref[place] = (align(raw_image, turn_ref[0, particle]) - predicted).astype(jnp.bfloat16)
        cross = lax.dot_general(
            raw_image, rounded, (((0,), (0,)), ((), ())), preferred_element_type=jnp.float32
        )
        turned = cross[:8]
        for tile in range(1, angles // 8):
            turned += pltpu.roll(cross[tile * 8 : tile * 8 + 8], angles - tile * 8, 1)
        spot = pl.ds(pl.multiple_of(particle * 8, 8), 8)
        folded[spot, :] = turned
        image_power[spot, :] = fold(image * image)
        predicted_power[spot, :] = fold(predicted * predicted)

    @pl.when(step == pl.num_programs(0) - 1)
    def _():
        number = folded.shape[0] // 8

        def part(ref, k):
            return ref[pl.ds(k, number, stride=8), :]

        corr = part(folded, 0)
        first = part(image_power, 0)
        second = part(predicted_power, 0)
        for k in range(1, 8):
            corr += pltpu.roll(part(folded, k), angles - k, 1)
            first += part(image_power, k)
            second += part(predicted_power, k)
        pixels = rows * angles
        ones = jnp.ones((1, angles), jnp.float32)

        def across(left, right, dims):
            return lax.dot_general(
                left, right, (dims, ((), ())), precision=HIGHEST, preferred_element_type=jnp.float32
            )

        first = jnp.sqrt(across(ones, first, ((1,), (1,))) / pixels + 1e-05)
        second = jnp.sqrt(across(ones, second, ((1,), (1,))) / pixels + 1e-05)
        turns = lax.broadcasted_iota(jnp.int32, (angles, angles), 1)
        shifts = lax.broadcasted_iota(jnp.int32, (angles, angles), 0)
        offset, one, two = mix(turns, angles)
        offset = lax.rem(offset, angles)
        table = jnp.where(shifts == offset, one, 0.0) + jnp.where(
            shifts == lax.rem(offset + 1, angles), two, 0.0
        )
        raw = across(table, corr, ((0,), (1,)))
        scores = raw / (math.sqrt(pixels) * first * second)
        scores_ref[...] = scores[:NROT].astype(jnp.bfloat16)


def body(particles, assign, rotation, group, ctf):
    images = particles[0]
    number, rows, angles = images.shape
    table = ctf.T
    shells = ctf.shape[1]
    count = lax.axis_size("cls")
    layers = count // QUAD
    steps = number // STEP
    cap = max(2, 2 * number // count)
    slots = count * cap
    params = pltpu.CompilerParams(vmem_limit_bytes=WIDE_BYTES)
    block = pl.BlockSpec((STEP, rows, angles), lambda i: (i, 0, 0))

    average, lever, partner = pl.pallas_call(
        functools.partial(share_kernel, count, cap),
        out_shape=(
            jax.ShapeDtypeStruct((rows, angles), jnp.bfloat16),
            jax.ShapeDtypeStruct((1, number), jnp.bfloat16),
            jax.ShapeDtypeStruct((count, rows, angles), jnp.bfloat16),
        ),
        in_specs=[anywhere()] * 5,
        out_specs=(vmem(), vmem(), pl.BlockSpec(memory_space=pl.ANY)),
        scratch_shapes=[
            pltpu.VMEM((number, rows, angles), jnp.bfloat16),
            pltpu.VMEM((1, number), jnp.int32),
            pltpu.SMEM((1, number), jnp.int32),
            pltpu.VMEM((1, number), jnp.int32),
            pltpu.VMEM(table.shape, jnp.float32),
            pltpu.VMEM((1, slots), jnp.int32),
            pltpu.SMEM((1, slots), jnp.int32),
            pltpu.VMEM((shells, slots), jnp.float32),
            pltpu.VMEM((count, rows, angles), jnp.bfloat16),
            pltpu.VMEM((layers, rows, angles), jnp.float32),
            pltpu.VMEM((1, 1, 2 * number), jnp.float32),
            pltpu.VMEM((count, 1, 2 * number), jnp.float32),
            pltpu.VMEM((count, rows, angles), jnp.bfloat16),
            pltpu.VMEM((layers, rows, angles), jnp.bfloat16),
            pltpu.VMEM((layers, rows, angles), jnp.bfloat16),
            pltpu.VMEM((rows, angles), jnp.bfloat16),
        ]
        + [pltpu.SemaphoreType.DMA((5,))]
        + [pltpu.SemaphoreType.DMA((count,))] * 4
        + [pltpu.SemaphoreType.DMA((layers,))] * 3
        + [pltpu.SemaphoreType.DMA((count,))] * 2,
        compiler_params=pltpu.CompilerParams(
            collective_id=0, has_side_effects=True, vmem_limit_bytes=WIDE_BYTES
        ),
        name="share",
    )(images, assign, rotation, group, table)

    residual, scores, average, lever = pl.pallas_call(
        compare_kernel,
        grid=(steps,),
        out_shape=(
            jax.ShapeDtypeStruct((number, rows, angles), jnp.bfloat16),
            jax.ShapeDtypeStruct((NROT, number), jnp.bfloat16),
            jax.ShapeDtypeStruct((rows, angles), jnp.bfloat16),
            jax.ShapeDtypeStruct((1, number), jnp.bfloat16),
        ),
        in_specs=[anywhere()] * 7 + [block],
        out_specs=(block, vmem(), vmem(), vmem()),
        scratch_shapes=[
            pltpu.SMEM((1, number), jnp.int32),
            pltpu.SMEM((1, number), jnp.int32),
            pltpu.VMEM((1, number), jnp.int32),
            pltpu.VMEM(table.shape, jnp.float32),
            pltpu.VMEM((count, rows, angles), jnp.bfloat16),
            pltpu.SemaphoreType.DMA((7,)),
            pltpu.VMEM((shells, 128), jnp.float32),
        ]
        + [pltpu.VMEM((number * 8, angles), jnp.float32)] * 3,
        compiler_params=params,
        name="compare",
    )(assign, rotation, group, table, partner, average, lever, images)
    return (average[None, None], residual[None], scores.T[None], lever)


def solution(mesh):
    in_specs = (
        P("half", "cls", None, None),
        P("half", "cls"),
        P("half", "cls"),
        P("half", "cls"),
        P(),
    )
    out_specs = (
        P("half", "cls", None, None),
        P("half", "cls", None, None),
        P("half", "cls", None),
        P("half", "cls"),
    )
    return jax.shard_map(body, mesh=mesh, in_specs=in_specs, out_specs=out_specs, check_vma=False)
```

```python
import functools
import math

import jax
import jax.numpy as jnp
import numpy as np
from jax import lax
from jax.experimental import pallas as pl
from jax.experimental.pallas import tpu as pltpu
from jax.sharding import PartitionSpec as P

NROT = 36
TAU = 1.0
STEP = 8
QUAD = 4
MESH = pl.DeviceIdType.MESH
HIGHEST = lax.Precision.HIGHEST
WIDE_BYTES = 62 * 1024 * 1024


def vmem():
    return pl.BlockSpec(memory_space=pltpu.VMEM)


def anywhere():
    return pl.BlockSpec(memory_space=pl.ANY)


def mix(turn, angles):
    scaled = turn * angles
    offset = scaled // NROT
    fraction = (scaled - offset * NROT).astype(jnp.float32) / NROT
    first = (1.0 - fraction).astype(jnp.bfloat16).astype(jnp.float32)
    second = fraction.astype(jnp.bfloat16).astype(jnp.float32)
    return offset, first, second


def rotation_table(angles):
    turns = np.arange(NROT)
    offset = turns * angles // NROT
    fraction = (turns * angles % NROT).astype(np.float32) / np.float32(NROT)
    table = np.zeros((NROT, angles, angles), np.float32)
    source = np.arange(angles)
    for r in range(NROT):
        table[r, source, (source + offset[r]) % angles] = np.float32(1.0) - fraction[r]
        table[r, source, (source + offset[r] + 1) % angles] = fraction[r]
    return jnp.asarray(table.astype(jnp.bfloat16))


def align(image, rotation):
    return jnp.dot(image, rotation, preferred_element_type=jnp.float32)


def one_hot(row, size):
    places = lax.broadcasted_iota(jnp.int32, (size, row.shape[1]), 0)
    return (places == row).astype(jnp.float32)


def columns_of(ctf, groups):
    return lax.dot_general(
        ctf,
        one_hot(groups, ctf.shape[1]),
        (((1,), (0,)), ((), ())),
        precision=HIGHEST,
        preferred_element_type=jnp.float32,
    )


def fill_columns(columns_ref, ctf_ref, group_ref):
    columns_ref[...] = jnp.zeros_like(columns_ref)
    columns_ref[:, : group_ref.shape[1]] = columns_of(ctf_ref[...], group_ref[...])


def step_columns(columns_ref, step):
    lanes = columns_ref.shape[1]
    return pltpu.roll(columns_ref[...], lax.rem(lanes - step * STEP, lanes), 1)


def stacked(columns, place, lanes):
    column = columns[:, place : place + 1]
    wide = jnp.broadcast_to(column, (columns.shape[0], lanes))
    return jnp.concatenate([wide, wide], axis=0)


def share_kernel(
    count,
    cap,
    images_hbm,
    assign_hbm,
    turn_hbm,
    group_hbm,
    ctf_hbm,
    table_hbm,
    average_ref,
    lever_ref,
    partner_ref,
    images_ref,
    assign_ref,
    turn_ref,
    group_ref,
    ctf_ref,
    table_ref,
    order_row,
    order_ref,
    slot_weights,
    sums_ref,
    own_sums,
    own_code,
    codes,
    landed,
    staged,
    gathered,
    average,
    loads,
    code_send,
    code_recv,
    quad_send,
    quad_recv,
    far_send,
    far_recv,
    avg_send,
    pass_send,
    avg_recv,
):
    half = lax.axis_index("half")
    me = lax.axis_index("cls")
    other = 1 - half
    layers = count // QUAD
    layer = me // QUAD
    spot = me % QUAD
    particles = assign_ref.shape[1]
    slots = count * cap

    pairs = (
        (assign_hbm, assign_ref),
        (group_hbm, group_ref),
        (ctf_hbm, ctf_ref),
        (turn_hbm, turn_ref),
        (images_hbm, images_ref),
        (table_hbm, table_ref),
    )
    moves = [pltpu.make_async_copy(a, b, loads.at[n]) for n, (a, b) in enumerate(pairs)]
    for move in moves:
        move.start()

    barrier = pltpu.get_barrier_semaphore()

    def greet(k, _):
        peer = lax.rem(me + k, count)
        pl.semaphore_signal(barrier, inc=1, device_id=(half, peer), device_id_type=MESH)
        return 0

    def greet_other(k, _):
        peer = lax.rem(layer + k, layers) * QUAD + spot
        pl.semaphore_signal(barrier, inc=1, device_id=(other, peer), device_id_type=MESH)
        return 0

    lax.fori_loop(1, count, greet, 0)
    lax.fori_loop(0, layers, greet_other, 0)
    for move in moves[:3]:
        move.wait()
    own_code[0] = jnp.concatenate([assign_ref[...], group_ref[...]], axis=1).astype(jnp.float32)
    line = lax.broadcasted_iota(jnp.int32, (particles, particles), 0)
    across = lax.broadcasted_iota(jnp.int32, (particles, particles), 1)

    def as_column(row):
        return jnp.sum(jnp.where(line == across, row, 0), axis=1, keepdims=True)

    same = (as_column(assign_ref[...]) == assign_ref[...]) & (line < across)
    rank = jnp.sum(jnp.where(same, 1, 0), axis=0, keepdims=True)
    places = assign_ref[...] * cap + rank
    taken = one_hot(places, slots)
    filled = as_column(places) == lax.broadcasted_iota(jnp.int32, (particles, slots), 1)
    numbers = lax.broadcasted_iota(jnp.int32, (particles, slots), 0)
    order_row[...] = jnp.sum(jnp.where(filled, numbers, 0), axis=0, keepdims=True)

    def to_slots(values):
        return lax.dot_general(
            values,
            taken,
            (((1,), (1,)), ((), ())),
            precision=HIGHEST,
            preferred_element_type=jnp.float32,
        )

    order_move = pltpu.make_async_copy(order_row, order_ref, loads.at[0])
    order_move.start()
    weights = columns_of(ctf_ref[...], group_ref[...])
    slot_weights[...] = to_slots(weights)
    order_move.wait()
    for move in moves[3:]:
        move.wait()
    pl.semaphore_wait(barrier, count - 1 + layers)

    def code_copy(source, peer):
        return pltpu.make_async_remote_copy(
            src_ref=own_code.at[0],
            dst_ref=codes.at[source],
            send_sem=code_send.at[peer],
            recv_sem=code_recv.at[source],
            device_id=(half, peer),
            device_id_type=MESH,
        )

    def quad_copy(level, source, target):
        return pltpu.make_async_remote_copy(
            src_ref=sums_ref.at[level * QUAD + target],
            dst_ref=landed.at[level * QUAD + source],
            send_sem=quad_send.at[level * QUAD + target],
            recv_sem=quad_recv.at[level * QUAD + source],
            device_id=(half, layer * QUAD + target),
            device_id_type=MESH,
        )

    def far_copy(source, target):
        return pltpu.make_async_remote_copy(
            src_ref=staged.at[target],
            dst_ref=gathered.at[source],
            send_sem=far_send.at[target],
            recv_sem=far_recv.at[source],
            device_id=(half, target * QUAD + spot),
            device_id_type=MESH,
        )

    def avg_copy(source, target):
        return pltpu.make_async_remote_copy(
            src_ref=average,
            dst_ref=partner_ref.at[source * QUAD + spot],
            send_sem=avg_send.at[target],
            recv_sem=avg_recv.at[source * QUAD + spot],
            device_id=(other, target * QUAD + spot),
            device_id_type=MESH,
        )

    def pass_copy(level, source, target):
        return pltpu.make_async_remote_copy(
            src_ref=partner_ref.at[level * QUAD + source],
            dst_ref=partner_ref.at[level * QUAD + source],
            send_sem=pass_send.at[level * QUAD + target],
            recv_sem=avg_recv.at[level * QUAD + source],
            device_id=(half, layer * QUAD + target),
            device_id_type=MESH,
        )

    def send_code(k, _):
        code_copy(me, lax.rem(me + k, count)).start()
        return 0

    lax.fori_loop(1, count, send_code, 0)

    def class_sum(owner):
        columns = pltpu.roll(slot_weights[...], lax.rem(slots - owner * cap, slots), 1)
        total = jnp.zeros(images_ref.shape[1:], jnp.float32)
        for place in range(cap):
            particle = jnp.clip(order_ref[0, owner * cap + place], 0, images_ref.shape[0] - 1)
            image = align(images_ref[particle], table_ref[turn_ref[0, particle]])
            total += stacked(columns, place, image.shape[1]) * image
        return total

    def quad_sum(level):
        total = own_sums[level]
        for j in range(1, QUAD):
            source = lax.rem(spot + j, QUAD)
            quad_copy(level, source, source).wait_recv()
            total += landed[level * QUAD + source].astype(jnp.float32)
        return total

    def send_far(k, _):
        level = lax.rem(layer + k, layers)
        staged[level] = quad_sum(level).astype(jnp.bfloat16)
        far_copy(layer, level).start()
        return 0

    def sum_level(k, _):
        level = lax.rem(layer + k, layers)
        for j in range(1, QUAD):
            target = lax.rem(spot + j, QUAD)
            sums_ref[level * QUAD + target] = class_sum(level * QUAD + target).astype(jnp.bfloat16)
            quad_copy(level, spot, target).start()
        own_sums[level] = class_sum(level * QUAD + spot)

        @pl.when(k > 1)
        def _():
            send_far(k - 1, 0)

        return 0

    lax.fori_loop(1, layers + 1, sum_level, 0)

    def tally(code):
        owners = one_hot(code[:, :particles].astype(jnp.int32), count)
        kinds = one_hot(code[:, particles:].astype(jnp.int32), ctf_ref.shape[1])
        return lax.dot_general(
            owners.astype(jnp.bfloat16),
            kinds.astype(jnp.bfloat16),
            (((1,), (1,)), ((), ())),
            preferred_element_type=jnp.float32,
        )

    def add_code(k, counts):
        source = lax.rem(me + count - k, count)
        return counts + tally(codes[source])

    def wait_code(k, _):
        source = lax.rem(me + count - k, count)
        code_copy(source, source).wait_recv()
        return 0

    lax.fori_loop(1, count, wait_code, 0)
    counts = lax.fori_loop(1, count, add_code, tally(own_code[0]), unroll=min(count - 1, 15))
    table = ctf_ref[...]
    den = lax.dot_general(
        table * table,
        counts,
        (((1,), (1,)), ((), ())),
        precision=HIGHEST,
        preferred_element_type=jnp.float32,
    )
    mine = lax.broadcasted_iota(jnp.int32, den.shape, 1) == me
    column = jnp.sum(jnp.where(mine, den, 0.0), axis=1, keepdims=True) + TAU
    denom = jnp.concatenate([column, column], axis=0)

    def add_far(k, total):
        source = lax.rem(layer + count - k, layers)
        far_copy(source, source).wait_recv()
        return total + gathered[source].astype(jnp.float32)

    total = lax.fori_loop(1, layers, add_far, quad_sum(layer))
    average[...] = (total / denom).astype(jnp.bfloat16)

    def send_avg(k, _):
        avg_copy(layer, lax.rem(layer + k, layers)).start()
        return 0

    lax.fori_loop(0, layers, send_avg, 0)
    average_ref[...] = average[...]
    chosen = jnp.dot(
        den,
        one_hot(assign_ref[...], count),
        precision=HIGHEST,
        preferred_element_type=jnp.float32,
    )
    lever = jnp.sum(weights * weights / (chosen + TAU), axis=0, keepdims=True)
    lever_ref[...] = (lever / table.shape[0]).astype(jnp.bfloat16)

    def pass_on(k, _):
        level = lax.rem(layer + k, layers)
        avg_copy(level, level).wait_recv()
        for j in range(1, QUAD):
            pass_copy(level, spot, lax.rem(spot + j, QUAD)).start()
        return 0

    lax.fori_loop(0, layers, pass_on, 0)

    def finish_code(k, _):
        code_copy(me, lax.rem(me + k, count)).wait_send()
        return 0

    def finish_far(k, _):
        far_copy(layer, lax.rem(layer + k, layers)).wait_send()
        return 0

    def finish_level(k, _):
        level = lax.rem(layer + k, layers)
        avg_copy(layer, level).wait_send()
        for j in range(1, QUAD):
            peer = lax.rem(spot + j, QUAD)
            quad_copy(level, spot, peer).wait_send()
            pass_copy(level, peer, peer).wait_recv()
            pass_copy(level, spot, peer).wait_send()
        return 0

    lax.fori_loop(1, count, finish_code, 0)
    lax.fori_loop(1, layers, finish_far, 0)
    lax.fori_loop(0, layers, finish_level, 0)


def compare_kernel(
    assign_hbm,
    turn_hbm,
    group_hbm,
    ctf_hbm,
    partner_hbm,
    average_hbm,
    lever_hbm,
    table_hbm,
    images_ref,
    residual_ref,
    scores_ref,
    average_out,
    lever_out,
    assign_ref,
    turn_ref,
    group_ref,
    ctf_ref,
    partner_ref,
    table_ref,
    loads,
    columns_ref,
    image_power,
    predicted_power,
    folded,
):
    step = pl.program_id(0)

    @pl.when(step == 0)
    def _():
        pairs = (
            (group_hbm, group_ref),
            (ctf_hbm, ctf_ref),
            (assign_hbm, assign_ref),
            (turn_hbm, turn_ref),
            (average_hbm, average_out),
            (lever_hbm, lever_out),
            (partner_hbm, partner_ref),
            (table_hbm, table_ref),
        )
        moves = [pltpu.make_async_copy(a, b, loads.at[n]) for n, (a, b) in enumerate(pairs)]
        for move in moves:
            move.start()
        for move in moves[:2]:
            move.wait()
        fill_columns(columns_ref, ctf_ref, group_ref)
        for move in moves[2:]:
            move.wait()

    columns = step_columns(columns_ref, step)
    rows, angles = images_ref.shape[1:]

    def fold(values):
        return jnp.sum(values.reshape(rows // 8, 8, angles), axis=0)

    for place in range(STEP):
        particle = step * STEP + place
        raw_image = images_ref[place]
        image = raw_image.astype(jnp.float32)
        weight = stacked(columns, place, angles)
        owner = assign_ref[0, particle]
        rounded = (weight * partner_ref[owner].astype(jnp.float32)).astype(jnp.bfloat16)
        predicted = rounded.astype(jnp.float32)
        residual_ref[place] = (align(raw_image, table_ref[turn_ref[0, particle]]) - predicted).astype(jnp.bfloat16)
        cross = lax.dot_general(
            raw_image, rounded, (((0,), (0,)), ((), ())), preferred_element_type=jnp.float32
        )
        turned = cross[:8]
        for tile in range(1, angles // 8):
            turned += pltpu.roll(cross[tile * 8 : tile * 8 + 8], angles - tile * 8, 1)
        spot = pl.ds(pl.multiple_of(particle * 8, 8), 8)
        folded[spot, :] = turned
        image_power[spot, :] = fold(image * image)
        predicted_power[spot, :] = fold(predicted * predicted)

    @pl.when(step == pl.num_programs(0) - 1)
    def _():
        number = folded.shape[0] // 8

        def part(ref, k):
            return ref[pl.ds(k, number, stride=8), :]

        corr = part(folded, 0)
        first = part(image_power, 0)
        second = part(predicted_power, 0)
        for k in range(1, 8):
            corr += pltpu.roll(part(folded, k), angles - k, 1)
            first += part(image_power, k)
            second += part(predicted_power, k)
        pixels = rows * angles
        ones = jnp.ones((1, angles), jnp.float32)

        def across(left, right, dims):
            return lax.dot_general(
                left, right, (dims, ((), ())), precision=HIGHEST, preferred_element_type=jnp.float32
            )

        first = jnp.sqrt(across(ones, first, ((1,), (1,))) / pixels + 1e-05)
        second = jnp.sqrt(across(ones, second, ((1,), (1,))) / pixels + 1e-05)
        turns = lax.broadcasted_iota(jnp.int32, (angles, angles), 1)
        shifts = lax.broadcasted_iota(jnp.int32, (angles, angles), 0)
        offset, one, two = mix(turns, angles)
        offset = lax.rem(offset, angles)
        table = jnp.where(shifts == offset, one, 0.0) + jnp.where(
            shifts == lax.rem(offset + 1, angles), two, 0.0
        )
        raw = across(table, corr, ((0,), (1,)))
        scores = raw / (math.sqrt(pixels) * first * second)
        scores_ref[...] = scores[:NROT].astype(jnp.bfloat16)


def body(particles, assign, rotation, group, ctf):
    images = particles[0]
    number, rows, angles = images.shape
    table = ctf.T
    rotations = rotation_table(angles)
    shells = ctf.shape[1]
    count = lax.axis_size("cls")
    layers = count // QUAD
    steps = number // STEP
    cap = max(2, 2 * number // count)
    slots = count * cap
    params = pltpu.CompilerParams(vmem_limit_bytes=WIDE_BYTES)
    block = pl.BlockSpec((STEP, rows, angles), lambda i: (i, 0, 0))

    average, lever, partner = pl.pallas_call(
        functools.partial(share_kernel, count, cap),
        out_shape=(
            jax.ShapeDtypeStruct((rows, angles), jnp.bfloat16),
            jax.ShapeDtypeStruct((1, number), jnp.bfloat16),
            jax.ShapeDtypeStruct((count, rows, angles), jnp.bfloat16),
        ),
        in_specs=[anywhere()] * 6,
        out_specs=(vmem(), vmem(), pl.BlockSpec(memory_space=pl.ANY)),
        scratch_shapes=[
            pltpu.VMEM((number, rows, angles), jnp.bfloat16),
            pltpu.VMEM((1, number), jnp.int32),
            pltpu.SMEM((1, number), jnp.int32),
            pltpu.VMEM((1, number), jnp.int32),
            pltpu.VMEM(table.shape, jnp.float32),
            pltpu.VMEM(rotations.shape, jnp.bfloat16),
            pltpu.VMEM((1, slots), jnp.int32),
            pltpu.SMEM((1, slots), jnp.int32),
            pltpu.VMEM((shells, slots), jnp.float32),
            pltpu.VMEM((count, rows, angles), jnp.bfloat16),
            pltpu.VMEM((layers, rows, angles), jnp.float32),
            pltpu.VMEM((1, 1, 2 * number), jnp.float32),
            pltpu.VMEM((count, 1, 2 * number), jnp.float32),
            pltpu.VMEM((count, rows, angles), jnp.bfloat16),
            pltpu.VMEM((layers, rows, angles), jnp.bfloat16),
            pltpu.VMEM((layers, rows, angles), jnp.bfloat16),
            pltpu.VMEM((rows, angles), jnp.bfloat16),
        ]
        + [pltpu.SemaphoreType.DMA((6,))]
        + [pltpu.SemaphoreType.DMA((count,))] * 4
        + [pltpu.SemaphoreType.DMA((layers,))] * 3
        + [pltpu.SemaphoreType.DMA((count,))] * 2,
        compiler_params=pltpu.CompilerParams(
            collective_id=0, has_side_effects=True, vmem_limit_bytes=WIDE_BYTES
        ),
        name="share",
    )(images, assign, rotation, group, table, rotations)

    residual, scores, average, lever = pl.pallas_call(
        compare_kernel,
        grid=(steps,),
        out_shape=(
            jax.ShapeDtypeStruct((number, rows, angles), jnp.bfloat16),
            jax.ShapeDtypeStruct((NROT, number), jnp.bfloat16),
            jax.ShapeDtypeStruct((rows, angles), jnp.bfloat16),
            jax.ShapeDtypeStruct((1, number), jnp.bfloat16),
        ),
        in_specs=[anywhere()] * 8 + [block],
        out_specs=(block, vmem(), vmem(), vmem()),
        scratch_shapes=[
            pltpu.SMEM((1, number), jnp.int32),
            pltpu.SMEM((1, number), jnp.int32),
            pltpu.VMEM((1, number), jnp.int32),
            pltpu.VMEM(table.shape, jnp.float32),
            pltpu.VMEM((count, rows, angles), jnp.bfloat16),
            pltpu.VMEM(rotations.shape, jnp.bfloat16),
            pltpu.SemaphoreType.DMA((8,)),
            pltpu.VMEM((shells, 128), jnp.float32),
        ]
        + [pltpu.VMEM((number * 8, angles), jnp.float32)] * 3,
        compiler_params=params,
        name="compare",
    )(assign, rotation, group, table, partner, average, lever, rotations, images)
    return (average[None, None], residual[None], scores.T[None], lever)


def solution(mesh):
    in_specs = (
        P("half", "cls", None, None),
        P("half", "cls"),
        P("half", "cls"),
        P("half", "cls"),
        P(),
    )
    out_specs = (
        P("half", "cls", None, None),
        P("half", "cls", None, None),
        P("half", "cls", None),
        P("half", "cls"),
    )
    return jax.shard_map(body, mesh=mesh, in_specs=in_specs, out_specs=out_specs, check_vma=False)
```

```python
import functools
import math

import jax
import jax.numpy as jnp
import numpy as np
from jax import lax
from jax.experimental import pallas as pl
from jax.experimental.pallas import tpu as pltpu
from jax.sharding import PartitionSpec as P

NROT = 36
TAU = 1.0
STEP = 8
BATCH = 4
QUAD = 4
MESH = pl.DeviceIdType.MESH
HIGHEST = lax.Precision.HIGHEST
WIDE_BYTES = 62 * 1024 * 1024


def vmem():
    return pl.BlockSpec(memory_space=pltpu.VMEM)


def anywhere():
    return pl.BlockSpec(memory_space=pl.ANY)


def mix(turn, angles):
    scaled = turn * angles
    offset = scaled // NROT
    fraction = (scaled - offset * NROT).astype(jnp.float32) / NROT
    first = (1.0 - fraction).astype(jnp.bfloat16).astype(jnp.float32)
    second = fraction.astype(jnp.bfloat16).astype(jnp.float32)
    return offset, first, second


def rotation_table(angles):
    turns = np.arange(NROT)
    offset = turns * angles // NROT
    fraction = (turns * angles % NROT).astype(np.float32) / np.float32(NROT)
    table = np.zeros((NROT, angles, angles), np.float32)
    source = np.arange(angles)
    for r in range(NROT):
        table[r, source, (source + offset[r]) % angles] = np.float32(1.0) - fraction[r]
        table[r, source, (source + offset[r] + 1) % angles] = fraction[r]
    return jnp.asarray(table.astype(jnp.bfloat16))


def align(image, rotation):
    return jnp.dot(image, rotation, preferred_element_type=jnp.float32)


def one_hot(row, size):
    places = lax.broadcasted_iota(jnp.int32, (size, row.shape[1]), 0)
    return (places == row).astype(jnp.float32)


def columns_of(ctf, groups):
    return lax.dot_general(
        ctf,
        one_hot(groups, ctf.shape[1]),
        (((1,), (0,)), ((), ())),
        precision=HIGHEST,
        preferred_element_type=jnp.float32,
    )


def fill_columns(columns_ref, ctf_ref, group_ref):
    columns_ref[...] = jnp.zeros_like(columns_ref)
    columns_ref[:, : group_ref.shape[1]] = columns_of(ctf_ref[...], group_ref[...])


def step_columns(columns_ref, step):
    lanes = columns_ref.shape[1]
    return pltpu.roll(columns_ref[...], lax.rem(lanes - step * STEP, lanes), 1)


def stacked(columns, place, lanes):
    column = columns[:, place : place + 1]
    wide = jnp.broadcast_to(column, (columns.shape[0], lanes))
    return jnp.concatenate([wide, wide], axis=0)


def share_kernel(
    count,
    cap,
    images_hbm,
    assign_hbm,
    turn_hbm,
    group_hbm,
    ctf_hbm,
    table_hbm,
    average_ref,
    lever_ref,
    partner_ref,
    images_ref,
    assign_ref,
    turn_ref,
    group_ref,
    ctf_ref,
    table_ref,
    order_row,
    order_ref,
    slot_weights,
    sums_ref,
    own_sums,
    own_code,
    codes,
    landed,
    staged,
    gathered,
    average,
    loads,
    code_send,
    code_recv,
    quad_send,
    quad_recv,
    far_send,
    far_recv,
    avg_send,
    pass_send,
    avg_recv,
):
    half = lax.axis_index("half")
    me = lax.axis_index("cls")
    other = 1 - half
    layers = count // QUAD
    layer = me // QUAD
    spot = me % QUAD
    particles = assign_ref.shape[1]
    slots = count * cap

    pairs = (
        (assign_hbm, assign_ref),
        (group_hbm, group_ref),
        (ctf_hbm, ctf_ref),
        (turn_hbm, turn_ref),
        (images_hbm, images_ref),
        (table_hbm, table_ref),
    )
    moves = [pltpu.make_async_copy(a, b, loads.at[n]) for n, (a, b) in enumerate(pairs)]
    for move in moves:
        move.start()

    barrier = pltpu.get_barrier_semaphore()

    def greet(k, _):
        peer = lax.rem(me + k, count)
        pl.semaphore_signal(barrier, inc=1, device_id=(half, peer), device_id_type=MESH)
        return 0

    def greet_other(k, _):
        peer = lax.rem(layer + k, layers) * QUAD + spot
        pl.semaphore_signal(barrier, inc=1, device_id=(other, peer), device_id_type=MESH)
        return 0

    lax.fori_loop(1, count, greet, 0)
    lax.fori_loop(0, layers, greet_other, 0)
    for move in moves[:3]:
        move.wait()
    own_code[0] = jnp.concatenate([assign_ref[...], group_ref[...]], axis=1).astype(jnp.float32)
    line = lax.broadcasted_iota(jnp.int32, (particles, particles), 0)
    across = lax.broadcasted_iota(jnp.int32, (particles, particles), 1)

    def as_column(row):
        return jnp.sum(jnp.where(line == across, row, 0), axis=1, keepdims=True)

    same = (as_column(assign_ref[...]) == assign_ref[...]) & (line < across)
    rank = jnp.sum(jnp.where(same, 1, 0), axis=0, keepdims=True)
    places = assign_ref[...] * cap + rank
    taken = one_hot(places, slots)
    filled = as_column(places) == lax.broadcasted_iota(jnp.int32, (particles, slots), 1)
    numbers = lax.broadcasted_iota(jnp.int32, (particles, slots), 0)
    order_row[...] = jnp.sum(jnp.where(filled, numbers, 0), axis=0, keepdims=True)

    def to_slots(values):
        return lax.dot_general(
            values,
            taken,
            (((1,), (1,)), ((), ())),
            precision=HIGHEST,
            preferred_element_type=jnp.float32,
        )

    order_move = pltpu.make_async_copy(order_row, order_ref, loads.at[0])
    order_move.start()
    weights = columns_of(ctf_ref[...], group_ref[...])
    slot_weights[...] = to_slots(weights)
    order_move.wait()
    for move in moves[3:]:
        move.wait()
    pl.semaphore_wait(barrier, count - 1 + layers)

    def code_copy(source, peer):
        return pltpu.make_async_remote_copy(
            src_ref=own_code.at[0],
            dst_ref=codes.at[source],
            send_sem=code_send.at[peer],
            recv_sem=code_recv.at[source],
            device_id=(half, peer),
            device_id_type=MESH,
        )

    def quad_copy(level, source, target):
        return pltpu.make_async_remote_copy(
            src_ref=sums_ref.at[level * QUAD + target],
            dst_ref=landed.at[level * QUAD + source],
            send_sem=quad_send.at[level * QUAD + target],
            recv_sem=quad_recv.at[level * QUAD + source],
            device_id=(half, layer * QUAD + target),
            device_id_type=MESH,
        )

    def far_copy(source, target):
        return pltpu.make_async_remote_copy(
            src_ref=staged.at[target],
            dst_ref=gathered.at[source],
            send_sem=far_send.at[target],
            recv_sem=far_recv.at[source],
            device_id=(half, target * QUAD + spot),
            device_id_type=MESH,
        )

    def avg_copy(source, target):
        return pltpu.make_async_remote_copy(
            src_ref=average,
            dst_ref=partner_ref.at[source * QUAD + spot],
            send_sem=avg_send.at[target],
            recv_sem=avg_recv.at[source * QUAD + spot],
            device_id=(other, target * QUAD + spot),
            device_id_type=MESH,
        )

    def pass_copy(level, source, target):
        return pltpu.make_async_remote_copy(
            src_ref=partner_ref.at[level * QUAD + source],
            dst_ref=partner_ref.at[level * QUAD + source],
            send_sem=pass_send.at[level * QUAD + target],
            recv_sem=avg_recv.at[level * QUAD + source],
            device_id=(half, layer * QUAD + target),
            device_id_type=MESH,
        )

    def send_code(k, _):
        code_copy(me, lax.rem(me + k, count)).start()
        return 0

    lax.fori_loop(1, count, send_code, 0)

    def class_sum(owner):
        columns = pltpu.roll(slot_weights[...], lax.rem(slots - owner * cap, slots), 1)
        total = jnp.zeros(images_ref.shape[1:], jnp.float32)
        for place in range(cap):
            particle = jnp.clip(order_ref[0, owner * cap + place], 0, images_ref.shape[0] - 1)
            image = align(images_ref[particle], table_ref[turn_ref[0, particle]])
            total += stacked(columns, place, image.shape[1]) * image
        return total

    def quad_sum(level):
        total = own_sums[level]
        for j in range(1, QUAD):
            source = lax.rem(spot + j, QUAD)
            quad_copy(level, source, source).wait_recv()
            total += landed[level * QUAD + source].astype(jnp.float32)
        return total

    def send_far(k, _):
        level = lax.rem(layer + k, layers)
        staged[level] = quad_sum(level).astype(jnp.bfloat16)
        far_copy(layer, level).start()
        return 0

    def sum_level(k, _):
        level = lax.rem(layer + k, layers)
        for pair in range(1, QUAD, 2):
            targets = [lax.rem(spot + j, QUAD) for j in (pair, pair + 1)]
            totals = [class_sum(level * QUAD + target) for target in targets]
            for j, target, total in zip((pair, pair + 1), targets, totals):
                if j < QUAD:
                    sums_ref[level * QUAD + target] = total.astype(jnp.bfloat16)
                    quad_copy(level, spot, target).start()
                else:
                    own_sums[level] = total

        @pl.when(k > 1)
        def _():
            send_far(k - 1, 0)

        return 0

    lax.fori_loop(1, layers + 1, sum_level, 0)

    def tally(code):
        owners = one_hot(code[:, :particles].astype(jnp.int32), count)
        kinds = one_hot(code[:, particles:].astype(jnp.int32), ctf_ref.shape[1])
        return lax.dot_general(
            owners.astype(jnp.bfloat16),
            kinds.astype(jnp.bfloat16),
            (((1,), (1,)), ((), ())),
            preferred_element_type=jnp.float32,
        )

    def add_code(k, counts):
        source = lax.rem(me + count - k, count)
        return counts + tally(codes[source])

    def wait_code(k, _):
        source = lax.rem(me + count - k, count)
        code_copy(source, source).wait_recv()
        return 0

    lax.fori_loop(1, count, wait_code, 0)
    counts = lax.fori_loop(1, count, add_code, tally(own_code[0]), unroll=min(count - 1, 15))
    table = ctf_ref[...]
    den = lax.dot_general(
        table * table,
        counts,
        (((1,), (1,)), ((), ())),
        precision=HIGHEST,
        preferred_element_type=jnp.float32,
    )
    mine = lax.broadcasted_iota(jnp.int32, den.shape, 1) == me
    column = jnp.sum(jnp.where(mine, den, 0.0), axis=1, keepdims=True) + TAU
    denom = jnp.concatenate([column, column], axis=0)

    def add_far(k, total):
        source = lax.rem(layer + count - k, layers)
        far_copy(source, source).wait_recv()
        return total + gathered[source].astype(jnp.float32)

    total = lax.fori_loop(1, layers, add_far, quad_sum(layer))
    average[...] = (total / denom).astype(jnp.bfloat16)

    def send_avg(k, _):
        avg_copy(layer, lax.rem(layer + k, layers)).start()
        return 0

    lax.fori_loop(0, layers, send_avg, 0)
    average_ref[...] = average[...]
    chosen = jnp.dot(
        den,
        one_hot(assign_ref[...], count),
        precision=HIGHEST,
        preferred_element_type=jnp.float32,
    )
    lever = jnp.sum(weights * weights / (chosen + TAU), axis=0, keepdims=True)
    lever_ref[...] = (lever / table.shape[0]).astype(jnp.bfloat16)

    def pass_on(k, _):
        level = lax.rem(layer + k, layers)
        avg_copy(level, level).wait_recv()
        for j in range(1, QUAD):
            pass_copy(level, spot, lax.rem(spot + j, QUAD)).start()
        return 0

    lax.fori_loop(0, layers, pass_on, 0)

    def finish_code(k, _):
        code_copy(me, lax.rem(me + k, count)).wait_send()
        return 0

    def finish_far(k, _):
        far_copy(layer, lax.rem(layer + k, layers)).wait_send()
        return 0

    def finish_level(k, _):
        level = lax.rem(layer + k, layers)
        avg_copy(layer, level).wait_send()
        for j in range(1, QUAD):
            peer = lax.rem(spot + j, QUAD)
            quad_copy(level, spot, peer).wait_send()
            pass_copy(level, peer, peer).wait_recv()
            pass_copy(level, spot, peer).wait_send()
        return 0

    lax.fori_loop(1, count, finish_code, 0)
    lax.fori_loop(1, layers, finish_far, 0)
    lax.fori_loop(0, layers, finish_level, 0)


def compare_kernel(
    assign_hbm,
    turn_hbm,
    group_hbm,
    ctf_hbm,
    partner_hbm,
    average_hbm,
    lever_hbm,
    table_hbm,
    images_ref,
    residual_ref,
    scores_ref,
    average_out,
    lever_out,
    assign_ref,
    turn_ref,
    group_ref,
    ctf_ref,
    partner_ref,
    table_ref,
    loads,
    columns_ref,
    image_power,
    predicted_power,
    folded,
):
    step = pl.program_id(0)

    @pl.when(step == 0)
    def _():
        pairs = (
            (group_hbm, group_ref),
            (ctf_hbm, ctf_ref),
            (assign_hbm, assign_ref),
            (turn_hbm, turn_ref),
            (average_hbm, average_out),
            (lever_hbm, lever_out),
            (partner_hbm, partner_ref),
            (table_hbm, table_ref),
        )
        moves = [pltpu.make_async_copy(a, b, loads.at[n]) for n, (a, b) in enumerate(pairs)]
        for move in moves:
            move.start()
        for move in moves[:2]:
            move.wait()
        fill_columns(columns_ref, ctf_ref, group_ref)
        for move in moves[2:]:
            move.wait()

    columns = step_columns(columns_ref, step)
    rows, angles = images_ref.shape[1:]

    def fold(values):
        return jnp.sum(values.reshape(rows // 8, 8, angles), axis=0)

    def work(place):
        particle = step * STEP + place
        raw_image = images_ref[place]
        image = raw_image.astype(jnp.float32)
        weight = stacked(columns, place, angles)
        owner = assign_ref[0, particle]
        rounded = (weight * partner_ref[owner].astype(jnp.float32)).astype(jnp.bfloat16)
        predicted = rounded.astype(jnp.float32)
        aligned = align(raw_image, table_ref[turn_ref[0, particle]])
        residual = (aligned - predicted).astype(jnp.bfloat16)
        cross = lax.dot_general(
            raw_image, rounded, (((0,), (0,)), ((), ())), preferred_element_type=jnp.float32
        )
        turned = cross[:8]
        for tile in range(1, angles // 8):
            turned += pltpu.roll(cross[tile * 8 : tile * 8 + 8], angles - tile * 8, 1)
        return residual, turned, fold(image * image), fold(predicted * predicted)

    for start in range(0, STEP, BATCH):
        places = range(start, start + BATCH)
        results = [work(place) for place in places]
        for place, (residual, turned, first, second) in zip(places, results):
            spot = pl.ds(pl.multiple_of((step * STEP + place) * 8, 8), 8)
            residual_ref[place] = residual
            folded[spot, :] = turned
            image_power[spot, :] = first
            predicted_power[spot, :] = second

    @pl.when(step == pl.num_programs(0) - 1)
    def _():
        number = folded.shape[0] // 8

        def part(ref, k):
            return ref[pl.ds(k, number, stride=8), :]

        corr = part(folded, 0)
        first = part(image_power, 0)
        second = part(predicted_power, 0)
        for k in range(1, 8):
            corr += pltpu.roll(part(folded, k), angles - k, 1)
            first += part(image_power, k)
            second += part(predicted_power, k)
        pixels = rows * angles
        ones = jnp.ones((1, angles), jnp.float32)

        def across(left, right, dims):
            return lax.dot_general(
                left, right, (dims, ((), ())), precision=HIGHEST, preferred_element_type=jnp.float32
            )

        first = jnp.sqrt(across(ones, first, ((1,), (1,))) / pixels + 1e-05)
        second = jnp.sqrt(across(ones, second, ((1,), (1,))) / pixels + 1e-05)
        turns = lax.broadcasted_iota(jnp.int32, (angles, angles), 1)
        shifts = lax.broadcasted_iota(jnp.int32, (angles, angles), 0)
        offset, one, two = mix(turns, angles)
        offset = lax.rem(offset, angles)
        table = jnp.where(shifts == offset, one, 0.0) + jnp.where(
            shifts == lax.rem(offset + 1, angles), two, 0.0
        )
        raw = across(table, corr, ((0,), (1,)))
        scores = raw / (math.sqrt(pixels) * first * second)
        scores_ref[...] = scores[:NROT].astype(jnp.bfloat16)


def body(particles, assign, rotation, group, ctf):
    images = particles[0]
    number, rows, angles = images.shape
    table = ctf.T
    rotations = rotation_table(angles)
    shells = ctf.shape[1]
    count = lax.axis_size("cls")
    layers = count // QUAD
    steps = number // STEP
    cap = max(2, 2 * number // count)
    slots = count * cap
    params = pltpu.CompilerParams(vmem_limit_bytes=WIDE_BYTES)
    block = pl.BlockSpec((STEP, rows, angles), lambda i: (i, 0, 0))

    average, lever, partner = pl.pallas_call(
        functools.partial(share_kernel, count, cap),
        out_shape=(
            jax.ShapeDtypeStruct((rows, angles), jnp.bfloat16),
            jax.ShapeDtypeStruct((1, number), jnp.bfloat16),
            jax.ShapeDtypeStruct((count, rows, angles), jnp.bfloat16),
        ),
        in_specs=[anywhere()] * 6,
        out_specs=(vmem(), vmem(), pl.BlockSpec(memory_space=pl.ANY)),
        scratch_shapes=[
            pltpu.VMEM((number, rows, angles), jnp.bfloat16),
            pltpu.VMEM((1, number), jnp.int32),
            pltpu.SMEM((1, number), jnp.int32),
            pltpu.VMEM((1, number), jnp.int32),
            pltpu.VMEM(table.shape, jnp.float32),
            pltpu.VMEM(rotations.shape, jnp.bfloat16),
            pltpu.VMEM((1, slots), jnp.int32),
            pltpu.SMEM((1, slots), jnp.int32),
            pltpu.VMEM((shells, slots), jnp.float32),
            pltpu.VMEM((count, rows, angles), jnp.bfloat16),
            pltpu.VMEM((layers, rows, angles), jnp.float32),
            pltpu.VMEM((1, 1, 2 * number), jnp.float32),
            pltpu.VMEM((count, 1, 2 * number), jnp.float32),
            pltpu.VMEM((count, rows, angles), jnp.bfloat16),
            pltpu.VMEM((layers, rows, angles), jnp.bfloat16),
            pltpu.VMEM((layers, rows, angles), jnp.bfloat16),
            pltpu.VMEM((rows, angles), jnp.bfloat16),
        ]
        + [pltpu.SemaphoreType.DMA((6,))]
        + [pltpu.SemaphoreType.DMA((count,))] * 4
        + [pltpu.SemaphoreType.DMA((layers,))] * 3
        + [pltpu.SemaphoreType.DMA((count,))] * 2,
        compiler_params=pltpu.CompilerParams(
            collective_id=0, has_side_effects=True, vmem_limit_bytes=WIDE_BYTES
        ),
        name="share",
    )(images, assign, rotation, group, table, rotations)

    residual, scores, average, lever = pl.pallas_call(
        compare_kernel,
        grid=(steps,),
        out_shape=(
            jax.ShapeDtypeStruct((number, rows, angles), jnp.bfloat16),
            jax.ShapeDtypeStruct((NROT, number), jnp.bfloat16),
            jax.ShapeDtypeStruct((rows, angles), jnp.bfloat16),
            jax.ShapeDtypeStruct((1, number), jnp.bfloat16),
        ),
        in_specs=[anywhere()] * 8 + [block],
        out_specs=(block, vmem(), vmem(), vmem()),
        scratch_shapes=[
            pltpu.SMEM((1, number), jnp.int32),
            pltpu.SMEM((1, number), jnp.int32),
            pltpu.VMEM((1, number), jnp.int32),
            pltpu.VMEM(table.shape, jnp.float32),
            pltpu.VMEM((count, rows, angles), jnp.bfloat16),
            pltpu.VMEM(rotations.shape, jnp.bfloat16),
            pltpu.SemaphoreType.DMA((8,)),
            pltpu.VMEM((shells, 128), jnp.float32),
        ]
        + [pltpu.VMEM((number * 8, angles), jnp.float32)] * 3,
        compiler_params=params,
        name="compare",
    )(assign, rotation, group, table, partner, average, lever, rotations, images)
    return (average[None, None], residual[None], scores.T[None], lever)


def solution(mesh):
    in_specs = (
        P("half", "cls", None, None),
        P("half", "cls"),
        P("half", "cls"),
        P("half", "cls"),
        P(),
    )
    out_specs = (
        P("half", "cls", None, None),
        P("half", "cls", None, None),
        P("half", "cls", None),
        P("half", "cls"),
    )
    return jax.shard_map(body, mesh=mesh, in_specs=in_specs, out_specs=out_specs, check_vma=False)
```

```python
import functools
import math

import jax
import jax.numpy as jnp
import numpy as np
from jax import lax
from jax.experimental import pallas as pl
from jax.experimental.pallas import tpu as pltpu
from jax.sharding import PartitionSpec as P

NROT = 36
TAU = 1.0
STEP = 8
BATCH = 4
CHUNK = 16
QUAD = 4
MESH = pl.DeviceIdType.MESH
HIGHEST = lax.Precision.HIGHEST
WIDE_BYTES = 62 * 1024 * 1024


def vmem():
    return pl.BlockSpec(memory_space=pltpu.VMEM)


def anywhere():
    return pl.BlockSpec(memory_space=pl.ANY)


def mix(turn, angles):
    scaled = turn * angles
    offset = scaled // NROT
    fraction = (scaled - offset * NROT).astype(jnp.float32) / NROT
    first = (1.0 - fraction).astype(jnp.bfloat16).astype(jnp.float32)
    second = fraction.astype(jnp.bfloat16).astype(jnp.float32)
    return offset, first, second


def rotation_table(angles):
    turns = np.arange(NROT)
    offset = turns * angles // NROT
    fraction = (turns * angles % NROT).astype(np.float32) / np.float32(NROT)
    table = np.zeros((NROT, angles, angles), np.float32)
    source = np.arange(angles)
    for r in range(NROT):
        table[r, source, (source + offset[r]) % angles] = np.float32(1.0) - fraction[r]
        table[r, source, (source + offset[r] + 1) % angles] = fraction[r]
    return jnp.asarray(table.astype(jnp.bfloat16))


def align(image, rotation):
    return jnp.dot(image, rotation, preferred_element_type=jnp.float32)


def one_hot(row, size):
    places = lax.broadcasted_iota(jnp.int32, (size, row.shape[1]), 0)
    return (places == row).astype(jnp.float32)


def columns_of(ctf, groups):
    return lax.dot_general(
        ctf,
        one_hot(groups, ctf.shape[1]),
        (((1,), (0,)), ((), ())),
        precision=HIGHEST,
        preferred_element_type=jnp.float32,
    )


def fill_columns(columns_ref, ctf_ref, group_ref):
    columns_ref[...] = jnp.zeros_like(columns_ref)
    columns_ref[:, : group_ref.shape[1]] = columns_of(ctf_ref[...], group_ref[...])


def step_columns(columns_ref, step):
    lanes = columns_ref.shape[1]
    return pltpu.roll(columns_ref[...], lax.rem(lanes - step * STEP, lanes), 1)


def stacked(columns, place, lanes):
    column = columns[:, place : place + 1]
    wide = jnp.broadcast_to(column, (columns.shape[0], lanes))
    return jnp.concatenate([wide, wide], axis=0)


def share_kernel(
    count,
    cap,
    images_hbm,
    assign_hbm,
    turn_hbm,
    group_hbm,
    ctf_hbm,
    table_hbm,
    average_ref,
    lever_ref,
    partner_ref,
    turned_hbm,
    images_ref,
    turned_ref,
    leave,
    assign_ref,
    turn_ref,
    group_ref,
    ctf_ref,
    table_ref,
    order_row,
    order_ref,
    slot_weights,
    sums_ref,
    own_sums,
    own_code,
    codes,
    landed,
    staged,
    gathered,
    average,
    loads,
    code_send,
    code_recv,
    quad_send,
    quad_recv,
    far_send,
    far_recv,
    avg_send,
    pass_send,
    avg_recv,
):
    half = lax.axis_index("half")
    me = lax.axis_index("cls")
    other = 1 - half
    layers = count // QUAD
    layer = me // QUAD
    spot = me % QUAD
    particles = assign_ref.shape[1]
    slots = count * cap

    pairs = (
        (assign_hbm, assign_ref),
        (group_hbm, group_ref),
        (ctf_hbm, ctf_ref),
        (turn_hbm, turn_ref),
        (images_hbm, images_ref),
        (table_hbm, table_ref),
    )
    moves = [pltpu.make_async_copy(a, b, loads.at[n]) for n, (a, b) in enumerate(pairs)]
    for move in moves:
        move.start()

    barrier = pltpu.get_barrier_semaphore()

    def greet(k, _):
        peer = lax.rem(me + k, count)
        pl.semaphore_signal(barrier, inc=1, device_id=(half, peer), device_id_type=MESH)
        return 0

    def greet_other(k, _):
        peer = lax.rem(layer + k, layers) * QUAD + spot
        pl.semaphore_signal(barrier, inc=1, device_id=(other, peer), device_id_type=MESH)
        return 0

    lax.fori_loop(1, count, greet, 0)
    lax.fori_loop(0, layers, greet_other, 0)
    for move in moves[:3]:
        move.wait()
    own_code[0] = jnp.concatenate([assign_ref[...], group_ref[...]], axis=1).astype(jnp.float32)
    line = lax.broadcasted_iota(jnp.int32, (particles, particles), 0)
    across = lax.broadcasted_iota(jnp.int32, (particles, particles), 1)

    def as_column(row):
        return jnp.sum(jnp.where(line == across, row, 0), axis=1, keepdims=True)

    same = (as_column(assign_ref[...]) == assign_ref[...]) & (line < across)
    rank = jnp.sum(jnp.where(same, 1, 0), axis=0, keepdims=True)
    places = assign_ref[...] * cap + rank
    taken = one_hot(places, slots)
    filled = as_column(places) == lax.broadcasted_iota(jnp.int32, (particles, slots), 1)
    numbers = lax.broadcasted_iota(jnp.int32, (particles, slots), 0)
    order_row[...] = jnp.sum(jnp.where(filled, numbers, 0), axis=0, keepdims=True)

    def to_slots(values):
        return lax.dot_general(
            values,
            taken,
            (((1,), (1,)), ((), ())),
            precision=HIGHEST,
            preferred_element_type=jnp.float32,
        )

    order_move = pltpu.make_async_copy(order_row, order_ref, loads.at[0])
    order_move.start()
    weights = columns_of(ctf_ref[...], group_ref[...])
    slot_weights[...] = to_slots(weights)
    order_move.wait()
    for move in moves[3:]:
        move.wait()
    pl.semaphore_wait(barrier, count - 1 + layers)

    def code_copy(source, peer):
        return pltpu.make_async_remote_copy(
            src_ref=own_code.at[0],
            dst_ref=codes.at[source],
            send_sem=code_send.at[peer],
            recv_sem=code_recv.at[source],
            device_id=(half, peer),
            device_id_type=MESH,
        )

    def quad_copy(level, source, target):
        return pltpu.make_async_remote_copy(
            src_ref=sums_ref.at[level * QUAD + target],
            dst_ref=landed.at[level * QUAD + source],
            send_sem=quad_send.at[level * QUAD + target],
            recv_sem=quad_recv.at[level * QUAD + source],
            device_id=(half, layer * QUAD + target),
            device_id_type=MESH,
        )

    def far_copy(source, target):
        return pltpu.make_async_remote_copy(
            src_ref=staged.at[target],
            dst_ref=gathered.at[source],
            send_sem=far_send.at[target],
            recv_sem=far_recv.at[source],
            device_id=(half, target * QUAD + spot),
            device_id_type=MESH,
        )

    def avg_copy(source, target):
        return pltpu.make_async_remote_copy(
            src_ref=average,
            dst_ref=partner_ref.at[source * QUAD + spot],
            send_sem=avg_send.at[target],
            recv_sem=avg_recv.at[source * QUAD + spot],
            device_id=(other, target * QUAD + spot),
            device_id_type=MESH,
        )

    def pass_copy(level, source, target):
        return pltpu.make_async_remote_copy(
            src_ref=partner_ref.at[level * QUAD + source],
            dst_ref=partner_ref.at[level * QUAD + source],
            send_sem=pass_send.at[level * QUAD + target],
            recv_sem=avg_recv.at[level * QUAD + source],
            device_id=(half, layer * QUAD + target),
            device_id_type=MESH,
        )


    def class_sum(owner):
        columns = pltpu.roll(slot_weights[...], lax.rem(slots - owner * cap, slots), 1)
        total = jnp.zeros(images_ref.shape[1:], jnp.float32)
        for place in range(cap):
            particle = jnp.clip(order_ref[0, owner * cap + place], 0, images_ref.shape[0] - 1)
            image = align(images_ref[particle], table_ref[turn_ref[0, particle]])
            total += stacked(columns, place, image.shape[1]) * image
        return total

    def quad_sum(level):
        total = own_sums[level]
        for j in range(1, QUAD):
            source = lax.rem(spot + j, QUAD)
            quad_copy(level, source, source).wait_recv()
            total += landed[level * QUAD + source].astype(jnp.float32)
        return total

    def send_far(k, _):
        level = lax.rem(layer + k, layers)
        staged[level] = quad_sum(level).astype(jnp.bfloat16)
        far_copy(layer, level).start()
        return 0

    def sum_level(k, _):
        level = lax.rem(layer + k, layers)
        for pair in range(1, QUAD, 2):
            targets = [lax.rem(spot + j, QUAD) for j in (pair, pair + 1)]
            totals = [class_sum(level * QUAD + target) for target in targets]
            for j, target, total in zip((pair, pair + 1), targets, totals):
                if j < QUAD:
                    sums_ref[level * QUAD + target] = total.astype(jnp.bfloat16)
                    quad_copy(level, spot, target).start()
                else:
                    own_sums[level] = total

        for j in range(1, QUAD):
            code_copy(me, level * QUAD + lax.rem(spot + j, QUAD)).start()

        @pl.when(k < layers)
        def _():
            code_copy(me, level * QUAD + spot).start()

        @pl.when(k > 1)
        def _():
            send_far(k - 1, 0)

        return 0

    lax.fori_loop(1, layers + 1, sum_level, 0)

    def tally(code):
        owners = one_hot(code[:, :particles].astype(jnp.int32), count)
        kinds = one_hot(code[:, particles:].astype(jnp.int32), ctf_ref.shape[1])
        return lax.dot_general(
            owners.astype(jnp.bfloat16),
            kinds.astype(jnp.bfloat16),
            (((1,), (1,)), ((), ())),
            preferred_element_type=jnp.float32,
        )

    def add_code(k, counts):
        source = lax.rem(me + count - k, count)
        return counts + tally(codes[source])

    def wait_code(k, _):
        source = lax.rem(me + count - k, count)
        code_copy(source, source).wait_recv()
        return 0

    lax.fori_loop(1, count, wait_code, 0)
    counts = lax.fori_loop(1, count, add_code, tally(own_code[0]), unroll=min(count - 1, 15))
    table = ctf_ref[...]
    den = lax.dot_general(
        table * table,
        counts,
        (((1,), (1,)), ((), ())),
        precision=HIGHEST,
        preferred_element_type=jnp.float32,
    )
    mine = lax.broadcasted_iota(jnp.int32, den.shape, 1) == me
    column = jnp.sum(jnp.where(mine, den, 0.0), axis=1, keepdims=True) + TAU
    denom = jnp.concatenate([column, column], axis=0)

    def add_far(k, total):
        source = lax.rem(layer + count - k, layers)
        far_copy(source, source).wait_recv()
        return total + gathered[source].astype(jnp.float32)

    total = lax.fori_loop(1, layers, add_far, quad_sum(layer))
    average[...] = (total / denom).astype(jnp.bfloat16)

    def send_avg(k, _):
        avg_copy(layer, lax.rem(layer + k, layers)).start()
        return 0

    lax.fori_loop(0, layers, send_avg, 0)
    average_ref[...] = average[...]
    chosen = jnp.dot(
        den,
        one_hot(assign_ref[...], count),
        precision=HIGHEST,
        preferred_element_type=jnp.float32,
    )
    lever = jnp.sum(weights * weights / (chosen + TAU), axis=0, keepdims=True)
    lever_ref[...] = (lever / table.shape[0]).astype(jnp.bfloat16)

    def pass_on(k, _):
        level = lax.rem(layer + k, layers)
        avg_copy(level, level).wait_recv()
        for j in range(1, QUAD):
            pass_copy(level, spot, lax.rem(spot + j, QUAD)).start()
        return 0

    lax.fori_loop(0, layers, pass_on, 0)

    def turned_move(chunk):
        piece = pl.ds(chunk * CHUNK, CHUNK)
        return pltpu.make_async_copy(turned_ref.at[piece], turned_hbm.at[piece], leave.at[chunk])

    def turn_chunk(chunk, _):
        for n in range(CHUNK):
            turned_ref[chunk * CHUNK + n] = images_ref[chunk * CHUNK + n].T
        turned_move(chunk).start()
        return 0

    chunks = particles // CHUNK
    lax.fori_loop(0, chunks, turn_chunk, 0)

    def finish_code(k, _):
        code_copy(me, lax.rem(me + k, count)).wait_send()
        return 0

    def finish_far(k, _):
        far_copy(layer, lax.rem(layer + k, layers)).wait_send()
        return 0

    def finish_level(k, _):
        level = lax.rem(layer + k, layers)
        avg_copy(layer, level).wait_send()
        for j in range(1, QUAD):
            peer = lax.rem(spot + j, QUAD)
            quad_copy(level, spot, peer).wait_send()
            pass_copy(level, peer, peer).wait_recv()
            pass_copy(level, spot, peer).wait_send()
        return 0

    lax.fori_loop(1, count, finish_code, 0)
    lax.fori_loop(1, layers, finish_far, 0)
    lax.fori_loop(0, layers, finish_level, 0)
    for chunk in range(chunks):
        turned_move(chunk).wait()


def compare_kernel(
    assign_hbm,
    turn_hbm,
    group_hbm,
    ctf_hbm,
    partner_hbm,
    average_hbm,
    lever_hbm,
    table_hbm,
    images_ref,
    turned_ref,
    residual_ref,
    scores_ref,
    average_out,
    lever_out,
    assign_ref,
    turn_ref,
    group_ref,
    ctf_ref,
    partner_ref,
    table_ref,
    loads,
    columns_ref,
    image_power,
    predicted_power,
    folded,
):
    step = pl.program_id(0)

    @pl.when(step == 0)
    def _():
        pairs = (
            (group_hbm, group_ref),
            (ctf_hbm, ctf_ref),
            (assign_hbm, assign_ref),
            (turn_hbm, turn_ref),
            (average_hbm, average_out),
            (lever_hbm, lever_out),
            (partner_hbm, partner_ref),
            (table_hbm, table_ref),
        )
        moves = [pltpu.make_async_copy(a, b, loads.at[n]) for n, (a, b) in enumerate(pairs)]
        for move in moves:
            move.start()
        for move in moves[:2]:
            move.wait()
        fill_columns(columns_ref, ctf_ref, group_ref)
        for move in moves[2:]:
            move.wait()

    columns = step_columns(columns_ref, step)
    rows, angles = images_ref.shape[1:]

    def fold(values):
        return jnp.sum(values.reshape(rows // 8, 8, angles), axis=0)

    def work(place):
        particle = step * STEP + place
        raw_image = images_ref[place]
        image = raw_image.astype(jnp.float32)
        weight = stacked(columns, place, angles)
        owner = assign_ref[0, particle]
        rounded = (weight * partner_ref[owner].astype(jnp.float32)).astype(jnp.bfloat16)
        predicted = rounded.astype(jnp.float32)
        aligned = align(raw_image, table_ref[turn_ref[0, particle]])
        residual = (aligned - predicted).astype(jnp.bfloat16)
        cross = jnp.dot(turned_ref[place], rounded, preferred_element_type=jnp.float32)
        turned = cross[:8]
        for tile in range(1, angles // 8):
            turned += pltpu.roll(cross[tile * 8 : tile * 8 + 8], angles - tile * 8, 1)
        return residual, turned, fold(image * image), fold(predicted * predicted)

    for start in range(0, STEP, BATCH):
        places = range(start, start + BATCH)
        results = [work(place) for place in places]
        for place, (residual, turned, first, second) in zip(places, results):
            spot = pl.ds(pl.multiple_of((step * STEP + place) * 8, 8), 8)
            residual_ref[place] = residual
            folded[spot, :] = turned
            image_power[spot, :] = first
            predicted_power[spot, :] = second

    @pl.when(step == pl.num_programs(0) - 1)
    def _():
        number = folded.shape[0] // 8

        def part(ref, k):
            return ref[pl.ds(k, number, stride=8), :]

        corr = part(folded, 0)
        first = part(image_power, 0)
        second = part(predicted_power, 0)
        for k in range(1, 8):
            corr += pltpu.roll(part(folded, k), angles - k, 1)
            first += part(image_power, k)
            second += part(predicted_power, k)
        pixels = rows * angles
        ones = jnp.ones((1, angles), jnp.float32)

        def across(left, right, dims):
            return lax.dot_general(
                left, right, (dims, ((), ())), precision=HIGHEST, preferred_element_type=jnp.float32
            )

        first = jnp.sqrt(across(ones, first, ((1,), (1,))) / pixels + 1e-05)
        second = jnp.sqrt(across(ones, second, ((1,), (1,))) / pixels + 1e-05)
        turns = lax.broadcasted_iota(jnp.int32, (angles, angles), 1)
        shifts = lax.broadcasted_iota(jnp.int32, (angles, angles), 0)
        offset, one, two = mix(turns, angles)
        offset = lax.rem(offset, angles)
        table = jnp.where(shifts == offset, one, 0.0) + jnp.where(
            shifts == lax.rem(offset + 1, angles), two, 0.0
        )
        raw = across(table, corr, ((0,), (1,)))
        scores = raw / (math.sqrt(pixels) * first * second)
        scores_ref[...] = scores[:NROT].astype(jnp.bfloat16)


def body(particles, assign, rotation, group, ctf):
    images = particles[0]
    number, rows, angles = images.shape
    table = ctf.T
    rotations = rotation_table(angles)
    shells = ctf.shape[1]
    count = lax.axis_size("cls")
    layers = count // QUAD
    steps = number // STEP
    cap = max(2, 2 * number // count)
    slots = count * cap
    params = pltpu.CompilerParams(vmem_limit_bytes=WIDE_BYTES)
    block = pl.BlockSpec((STEP, rows, angles), lambda i: (i, 0, 0))
    flipped = pl.BlockSpec((STEP, angles, rows), lambda i: (i, 0, 0))

    average, lever, partner, turned = pl.pallas_call(
        functools.partial(share_kernel, count, cap),
        out_shape=(
            jax.ShapeDtypeStruct((rows, angles), jnp.bfloat16),
            jax.ShapeDtypeStruct((1, number), jnp.bfloat16),
            jax.ShapeDtypeStruct((count, rows, angles), jnp.bfloat16),
            jax.ShapeDtypeStruct((number, angles, rows), jnp.bfloat16),
        ),
        in_specs=[anywhere()] * 6,
        out_specs=(vmem(), vmem(), anywhere(), anywhere()),
        scratch_shapes=[
            pltpu.VMEM((number, rows, angles), jnp.bfloat16),
            pltpu.VMEM((number, angles, rows), jnp.bfloat16),
            pltpu.SemaphoreType.DMA((number // CHUNK,)),
            pltpu.VMEM((1, number), jnp.int32),
            pltpu.SMEM((1, number), jnp.int32),
            pltpu.VMEM((1, number), jnp.int32),
            pltpu.VMEM(table.shape, jnp.float32),
            pltpu.VMEM(rotations.shape, jnp.bfloat16),
            pltpu.VMEM((1, slots), jnp.int32),
            pltpu.SMEM((1, slots), jnp.int32),
            pltpu.VMEM((shells, slots), jnp.float32),
            pltpu.VMEM((count, rows, angles), jnp.bfloat16),
            pltpu.VMEM((layers, rows, angles), jnp.float32),
            pltpu.VMEM((1, 1, 2 * number), jnp.float32),
            pltpu.VMEM((count, 1, 2 * number), jnp.float32),
            pltpu.VMEM((count, rows, angles), jnp.bfloat16),
            pltpu.VMEM((layers, rows, angles), jnp.bfloat16),
            pltpu.VMEM((layers, rows, angles), jnp.bfloat16),
            pltpu.VMEM((rows, angles), jnp.bfloat16),
        ]
        + [pltpu.SemaphoreType.DMA((6,))]
        + [pltpu.SemaphoreType.DMA((count,))] * 4
        + [pltpu.SemaphoreType.DMA((layers,))] * 3
        + [pltpu.SemaphoreType.DMA((count,))] * 2,
        compiler_params=pltpu.CompilerParams(
            collective_id=0, has_side_effects=True, vmem_limit_bytes=WIDE_BYTES
        ),
        name="share",
    )(images, assign, rotation, group, table, rotations)

    residual, scores, average, lever = pl.pallas_call(
        compare_kernel,
        grid=(steps,),
        out_shape=(
            jax.ShapeDtypeStruct((number, rows, angles), jnp.bfloat16),
            jax.ShapeDtypeStruct((NROT, number), jnp.bfloat16),
            jax.ShapeDtypeStruct((rows, angles), jnp.bfloat16),
            jax.ShapeDtypeStruct((1, number), jnp.bfloat16),
        ),
        in_specs=[anywhere()] * 8 + [block, flipped],
        out_specs=(block, vmem(), vmem(), vmem()),
        scratch_shapes=[
            pltpu.SMEM((1, number), jnp.int32),
            pltpu.SMEM((1, number), jnp.int32),
            pltpu.VMEM((1, number), jnp.int32),
            pltpu.VMEM(table.shape, jnp.float32),
            pltpu.VMEM((count, rows, angles), jnp.bfloat16),
            pltpu.VMEM(rotations.shape, jnp.bfloat16),
            pltpu.SemaphoreType.DMA((8,)),
            pltpu.VMEM((shells, 128), jnp.float32),
        ]
        + [pltpu.VMEM((number * 8, angles), jnp.float32)] * 3,
        compiler_params=params,
        name="compare",
    )(assign, rotation, group, table, partner, average, lever, rotations, images, turned)
    return (average[None, None], residual[None], scores.T[None], lever)


def solution(mesh):
    in_specs = (
        P("half", "cls", None, None),
        P("half", "cls"),
        P("half", "cls"),
        P("half", "cls"),
        P(),
    )
    out_specs = (
        P("half", "cls", None, None),
        P("half", "cls", None, None),
        P("half", "cls", None),
        P("half", "cls"),
    )
    return jax.shard_map(body, mesh=mesh, in_specs=in_specs, out_specs=out_specs, check_vma=False)
```

```python
import functools
import math

import jax
import jax.numpy as jnp
import numpy as np
from jax import lax
from jax.experimental import pallas as pl
from jax.experimental.pallas import tpu as pltpu
from jax.sharding import PartitionSpec as P

NROT = 36
TAU = 1.0
STEP = 16
BATCH = 4
QUAD = 4
MESH = pl.DeviceIdType.MESH
HIGHEST = lax.Precision.HIGHEST
WIDE_BYTES = 62 * 1024 * 1024


def vmem():
    return pl.BlockSpec(memory_space=pltpu.VMEM)


def anywhere():
    return pl.BlockSpec(memory_space=pl.ANY)


def mix(turn, angles):
    scaled = turn * angles
    offset = scaled // NROT
    fraction = (scaled - offset * NROT).astype(jnp.float32) / NROT
    first = (1.0 - fraction).astype(jnp.bfloat16).astype(jnp.float32)
    second = fraction.astype(jnp.bfloat16).astype(jnp.float32)
    return offset, first, second


def rotation_table(angles):
    turns = np.arange(NROT)
    offset = turns * angles // NROT
    fraction = (turns * angles % NROT).astype(np.float32) / np.float32(NROT)
    table = np.zeros((NROT, angles, angles), np.float32)
    source = np.arange(angles)
    for r in range(NROT):
        table[r, source, (source + offset[r]) % angles] = np.float32(1.0) - fraction[r]
        table[r, source, (source + offset[r] + 1) % angles] = fraction[r]
    return jnp.asarray(table.astype(jnp.bfloat16))


def align(image, rotation):
    return jnp.dot(image, rotation, preferred_element_type=jnp.float32)


def one_hot(row, size):
    places = lax.broadcasted_iota(jnp.int32, (size, row.shape[1]), 0)
    return (places == row).astype(jnp.float32)


def columns_of(ctf, groups):
    return lax.dot_general(
        ctf,
        one_hot(groups, ctf.shape[1]),
        (((1,), (0,)), ((), ())),
        precision=HIGHEST,
        preferred_element_type=jnp.float32,
    )


def fill_columns(columns_ref, ctf_ref, group_ref):
    columns_ref[...] = jnp.zeros_like(columns_ref)
    columns_ref[:, : group_ref.shape[1]] = columns_of(ctf_ref[...], group_ref[...])


def step_columns(columns_ref, step):
    lanes = columns_ref.shape[1]
    return pltpu.roll(columns_ref[...], lax.rem(lanes - step * STEP, lanes), 1)


def stacked(columns, place, lanes):
    column = columns[:, place : place + 1]
    wide = jnp.broadcast_to(column, (columns.shape[0], lanes))
    return jnp.concatenate([wide, wide], axis=0)


def share_kernel(
    count,
    cap,
    images_hbm,
    assign_hbm,
    turn_hbm,
    group_hbm,
    ctf_hbm,
    table_hbm,
    average_ref,
    lever_ref,
    partner_ref,
    images_ref,
    assign_ref,
    turn_ref,
    group_ref,
    ctf_ref,
    table_ref,
    order_row,
    order_ref,
    slot_weights,
    sums_ref,
    own_sums,
    own_code,
    codes,
    landed,
    staged,
    gathered,
    average,
    loads,
    code_send,
    code_recv,
    quad_send,
    quad_recv,
    far_send,
    far_recv,
    avg_send,
    pass_send,
    avg_recv,
):
    half = lax.axis_index("half")
    me = lax.axis_index("cls")
    other = 1 - half
    layers = count // QUAD
    layer = me // QUAD
    spot = me % QUAD
    particles = assign_ref.shape[1]
    slots = count * cap

    pairs = (
        (assign_hbm, assign_ref),
        (group_hbm, group_ref),
        (ctf_hbm, ctf_ref),
        (turn_hbm, turn_ref),
        (images_hbm, images_ref),
        (table_hbm, table_ref),
    )
    moves = [pltpu.make_async_copy(a, b, loads.at[n]) for n, (a, b) in enumerate(pairs)]
    for move in moves:
        move.start()

    barrier = pltpu.get_barrier_semaphore()

    def greet(k, _):
        peer = lax.rem(me + k, count)
        pl.semaphore_signal(barrier, inc=1, device_id=(half, peer), device_id_type=MESH)
        return 0

    def greet_other(k, _):
        peer = lax.rem(layer + k, layers) * QUAD + spot
        pl.semaphore_signal(barrier, inc=1, device_id=(other, peer), device_id_type=MESH)
        return 0

    lax.fori_loop(1, count, greet, 0)
    lax.fori_loop(0, layers, greet_other, 0)
    for move in moves[:3]:
        move.wait()
    own_code[0] = jnp.concatenate([assign_ref[...], group_ref[...]], axis=1).astype(jnp.float32)
    line = lax.broadcasted_iota(jnp.int32, (particles, particles), 0)
    across = lax.broadcasted_iota(jnp.int32, (particles, particles), 1)

    def as_column(row):
        return jnp.sum(jnp.where(line == across, row, 0), axis=1, keepdims=True)

    same = (as_column(assign_ref[...]) == assign_ref[...]) & (line < across)
    rank = jnp.sum(jnp.where(same, 1, 0), axis=0, keepdims=True)
    places = assign_ref[...] * cap + rank
    taken = one_hot(places, slots)
    filled = as_column(places) == lax.broadcasted_iota(jnp.int32, (particles, slots), 1)
    numbers = lax.broadcasted_iota(jnp.int32, (particles, slots), 0)
    order_row[...] = jnp.sum(jnp.where(filled, numbers, 0), axis=0, keepdims=True)

    def to_slots(values):
        return lax.dot_general(
            values,
            taken,
            (((1,), (1,)), ((), ())),
            precision=HIGHEST,
            preferred_element_type=jnp.float32,
        )

    order_move = pltpu.make_async_copy(order_row, order_ref, loads.at[0])
    order_move.start()
    weights = columns_of(ctf_ref[...], group_ref[...])
    slot_weights[...] = to_slots(weights)
    order_move.wait()
    for move in moves[3:]:
        move.wait()
    pl.semaphore_wait(barrier, count - 1 + layers)

    def code_copy(source, peer):
        return pltpu.make_async_remote_copy(
            src_ref=own_code.at[0],
            dst_ref=codes.at[source],
            send_sem=code_send.at[peer],
            recv_sem=code_recv.at[source],
            device_id=(half, peer),
            device_id_type=MESH,
        )

    def quad_copy(level, source, target):
        return pltpu.make_async_remote_copy(
            src_ref=sums_ref.at[level * QUAD + target],
            dst_ref=landed.at[level * QUAD + source],
            send_sem=quad_send.at[level * QUAD + target],
            recv_sem=quad_recv.at[level * QUAD + source],
            device_id=(half, layer * QUAD + target),
            device_id_type=MESH,
        )

    def far_copy(source, target):
        return pltpu.make_async_remote_copy(
            src_ref=staged.at[target],
            dst_ref=gathered.at[source],
            send_sem=far_send.at[target],
            recv_sem=far_recv.at[source],
            device_id=(half, target * QUAD + spot),
            device_id_type=MESH,
        )

    def avg_copy(source, target):
        return pltpu.make_async_remote_copy(
            src_ref=average,
            dst_ref=partner_ref.at[source * QUAD + spot],
            send_sem=avg_send.at[target],
            recv_sem=avg_recv.at[source * QUAD + spot],
            device_id=(other, target * QUAD + spot),
            device_id_type=MESH,
        )

    def pass_copy(level, source, target):
        return pltpu.make_async_remote_copy(
            src_ref=partner_ref.at[level * QUAD + source],
            dst_ref=partner_ref.at[level * QUAD + source],
            send_sem=pass_send.at[level * QUAD + target],
            recv_sem=avg_recv.at[level * QUAD + source],
            device_id=(half, layer * QUAD + target),
            device_id_type=MESH,
        )


    def class_sum(owner):
        columns = pltpu.roll(slot_weights[...], lax.rem(slots - owner * cap, slots), 1)
        total = jnp.zeros(images_ref.shape[1:], jnp.float32)
        for place in range(cap):
            particle = jnp.clip(order_ref[0, owner * cap + place], 0, images_ref.shape[0] - 1)
            image = align(images_ref[particle], table_ref[turn_ref[0, particle]])
            total += stacked(columns, place, image.shape[1]) * image
        return total

    def quad_sum(level):
        total = own_sums[level]
        for j in range(1, QUAD):
            source = lax.rem(spot + j, QUAD)
            quad_copy(level, source, source).wait_recv()
            total += landed[level * QUAD + source].astype(jnp.float32)
        return total

    def send_far(k, _):
        level = lax.rem(layer + k, layers)
        staged[level] = quad_sum(level).astype(jnp.bfloat16)
        far_copy(layer, level).start()
        return 0

    def sum_level(k, _):
        level = lax.rem(layer + k, layers)
        for pair in range(1, QUAD, 2):
            targets = [lax.rem(spot + j, QUAD) for j in (pair, pair + 1)]
            totals = [class_sum(level * QUAD + target) for target in targets]
            for j, target, total in zip((pair, pair + 1), targets, totals):
                if j < QUAD:
                    sums_ref[level * QUAD + target] = total.astype(jnp.bfloat16)
                    quad_copy(level, spot, target).start()
                else:
                    own_sums[level] = total

        for j in range(1, QUAD):
            code_copy(me, level * QUAD + lax.rem(spot + j, QUAD)).start()

        @pl.when(k < layers)
        def _():
            code_copy(me, level * QUAD + spot).start()

        @pl.when(k > 1)
        def _():
            send_far(k - 1, 0)

        return 0

    lax.fori_loop(1, layers + 1, sum_level, 0)

    def tally(code):
        owners = one_hot(code[:, :particles].astype(jnp.int32), count)
        kinds = one_hot(code[:, particles:].astype(jnp.int32), ctf_ref.shape[1])
        return lax.dot_general(
            owners.astype(jnp.bfloat16),
            kinds.astype(jnp.bfloat16),
            (((1,), (1,)), ((), ())),
            preferred_element_type=jnp.float32,
        )

    def add_code(k, counts):
        source = lax.rem(me + count - k, count)
        return counts + tally(codes[source])

    def wait_code(k, _):
        source = lax.rem(me + count - k, count)
        code_copy(source, source).wait_recv()
        return 0

    lax.fori_loop(1, count, wait_code, 0)
    counts = lax.fori_loop(1, count, add_code, tally(own_code[0]), unroll=min(count - 1, 15))
    table = ctf_ref[...]
    den = lax.dot_general(
        table * table,
        counts,
        (((1,), (1,)), ((), ())),
        precision=HIGHEST,
        preferred_element_type=jnp.float32,
    )
    mine = lax.broadcasted_iota(jnp.int32, den.shape, 1) == me
    column = jnp.sum(jnp.where(mine, den, 0.0), axis=1, keepdims=True) + TAU
    denom = jnp.concatenate([column, column], axis=0)

    def add_far(k, total):
        source = lax.rem(layer + count - k, layers)
        far_copy(source, source).wait_recv()
        return total + gathered[source].astype(jnp.float32)

    total = lax.fori_loop(1, layers, add_far, quad_sum(layer))
    average[...] = (total / denom).astype(jnp.bfloat16)

    def send_avg(k, _):
        avg_copy(layer, lax.rem(layer + k, layers)).start()
        return 0

    lax.fori_loop(0, layers, send_avg, 0)
    average_ref[...] = average[...]
    chosen = jnp.dot(
        den,
        one_hot(assign_ref[...], count),
        precision=HIGHEST,
        preferred_element_type=jnp.float32,
    )
    lever = jnp.sum(weights * weights / (chosen + TAU), axis=0, keepdims=True)
    lever_ref[...] = (lever / table.shape[0]).astype(jnp.bfloat16)

    def pass_on(k, _):
        level = lax.rem(layer + k, layers)
        avg_copy(level, level).wait_recv()
        for j in range(1, QUAD):
            pass_copy(level, spot, lax.rem(spot + j, QUAD)).start()
        return 0

    lax.fori_loop(0, layers, pass_on, 0)

    def finish_code(k, _):
        code_copy(me, lax.rem(me + k, count)).wait_send()
        return 0

    def finish_far(k, _):
        far_copy(layer, lax.rem(layer + k, layers)).wait_send()
        return 0

    def finish_level(k, _):
        level = lax.rem(layer + k, layers)
        avg_copy(layer, level).wait_send()
        for j in range(1, QUAD):
            peer = lax.rem(spot + j, QUAD)
            quad_copy(level, spot, peer).wait_send()
            pass_copy(level, peer, peer).wait_recv()
            pass_copy(level, spot, peer).wait_send()
        return 0

    lax.fori_loop(1, count, finish_code, 0)
    lax.fori_loop(1, layers, finish_far, 0)
    lax.fori_loop(0, layers, finish_level, 0)


def compare_kernel(
    assign_hbm,
    turn_hbm,
    group_hbm,
    ctf_hbm,
    partner_hbm,
    average_hbm,
    lever_hbm,
    table_hbm,
    images_ref,
    residual_ref,
    scores_ref,
    average_out,
    lever_out,
    assign_ref,
    turn_ref,
    group_ref,
    ctf_ref,
    partner_ref,
    table_ref,
    loads,
    columns_ref,
    image_power,
    predicted_power,
    folded,
):
    step = pl.program_id(0)

    @pl.when(step == 0)
    def _():
        pairs = (
            (group_hbm, group_ref),
            (ctf_hbm, ctf_ref),
            (assign_hbm, assign_ref),
            (turn_hbm, turn_ref),
            (average_hbm, average_out),
            (lever_hbm, lever_out),
            (partner_hbm, partner_ref),
            (table_hbm, table_ref),
        )
        moves = [pltpu.make_async_copy(a, b, loads.at[n]) for n, (a, b) in enumerate(pairs)]
        for move in moves:
            move.start()
        for move in moves[:2]:
            move.wait()
        fill_columns(columns_ref, ctf_ref, group_ref)
        for move in moves[2:]:
            move.wait()

    columns = step_columns(columns_ref, step)
    rows, angles = images_ref.shape[1:]

    def fold(values):
        return jnp.sum(values.reshape(rows // 8, 8, angles), axis=0)

    def work(place):
        particle = step * STEP + place
        raw_image = images_ref[place]
        image = raw_image.astype(jnp.float32)
        weight = stacked(columns, place, angles)
        owner = assign_ref[0, particle]
        rounded = (weight * partner_ref[owner].astype(jnp.float32)).astype(jnp.bfloat16)
        predicted = rounded.astype(jnp.float32)
        aligned = align(raw_image, table_ref[turn_ref[0, particle]])
        residual = (aligned - predicted).astype(jnp.bfloat16)
        cross = lax.dot_general(
            raw_image, rounded, (((0,), (0,)), ((), ())), preferred_element_type=jnp.float32
        )
        turned = cross[:8]
        for tile in range(1, angles // 8):
            turned += pltpu.roll(cross[tile * 8 : tile * 8 + 8], angles - tile * 8, 1)
        return residual, turned, fold(image * image), fold(predicted * predicted)

    for start in range(0, STEP, BATCH):
        places = range(start, start + BATCH)
        results = [work(place) for place in places]
        for place, (residual, turned, first, second) in zip(places, results):
            spot = pl.ds(pl.multiple_of((step * STEP + place) * 8, 8), 8)
            residual_ref[place] = residual
            folded[spot, :] = turned
            image_power[spot, :] = first
            predicted_power[spot, :] = second

    @pl.when(step == pl.num_programs(0) - 1)
    def _():
        number = folded.shape[0] // 8

        def part(ref, k):
            return ref[pl.ds(k, number, stride=8), :]

        corr = part(folded, 0)
        first = part(image_power, 0)
        second = part(predicted_power, 0)
        for k in range(1, 8):
            corr += pltpu.roll(part(folded, k), angles - k, 1)
            first += part(image_power, k)
            second += part(predicted_power, k)
        pixels = rows * angles
        ones = jnp.ones((1, angles), jnp.float32)

        def across(left, right, dims):
            return lax.dot_general(
                left, right, (dims, ((), ())), precision=HIGHEST, preferred_element_type=jnp.float32
            )

        first = jnp.sqrt(across(ones, first, ((1,), (1,))) / pixels + 1e-05)
        second = jnp.sqrt(across(ones, second, ((1,), (1,))) / pixels + 1e-05)
        turns = lax.broadcasted_iota(jnp.int32, (angles, angles), 1)
        shifts = lax.broadcasted_iota(jnp.int32, (angles, angles), 0)
        offset, one, two = mix(turns, angles)
        offset = lax.rem(offset, angles)
        table = jnp.where(shifts == offset, one, 0.0) + jnp.where(
            shifts == lax.rem(offset + 1, angles), two, 0.0
        )
        raw = across(table, corr, ((0,), (1,)))
        scores = raw / (math.sqrt(pixels) * first * second)
        scores_ref[...] = scores[:NROT].astype(jnp.bfloat16)


def body(particles, assign, rotation, group, ctf):
    images = particles[0]
    number, rows, angles = images.shape
    table = ctf.T
    rotations = rotation_table(angles)
    shells = ctf.shape[1]
    count = lax.axis_size("cls")
    layers = count // QUAD
    steps = number // STEP
    cap = max(2, 2 * number // count)
    slots = count * cap
    params = pltpu.CompilerParams(vmem_limit_bytes=WIDE_BYTES)
    block = pl.BlockSpec((STEP, rows, angles), lambda i: (i, 0, 0))

    average, lever, partner = pl.pallas_call(
        functools.partial(share_kernel, count, cap),
        out_shape=(
            jax.ShapeDtypeStruct((rows, angles), jnp.bfloat16),
            jax.ShapeDtypeStruct((1, number), jnp.bfloat16),
            jax.ShapeDtypeStruct((count, rows, angles), jnp.bfloat16),
        ),
        in_specs=[anywhere()] * 6,
        out_specs=(vmem(), vmem(), pl.BlockSpec(memory_space=pl.ANY)),
        scratch_shapes=[
            pltpu.VMEM((number, rows, angles), jnp.bfloat16),
            pltpu.VMEM((1, number), jnp.int32),
            pltpu.SMEM((1, number), jnp.int32),
            pltpu.VMEM((1, number), jnp.int32),
            pltpu.VMEM(table.shape, jnp.float32),
            pltpu.VMEM(rotations.shape, jnp.bfloat16),
            pltpu.VMEM((1, slots), jnp.int32),
            pltpu.SMEM((1, slots), jnp.int32),
            pltpu.VMEM((shells, slots), jnp.float32),
            pltpu.VMEM((count, rows, angles), jnp.bfloat16),
            pltpu.VMEM((layers, rows, angles), jnp.float32),
            pltpu.VMEM((1, 1, 2 * number), jnp.float32),
            pltpu.VMEM((count, 1, 2 * number), jnp.float32),
            pltpu.VMEM((count, rows, angles), jnp.bfloat16),
            pltpu.VMEM((layers, rows, angles), jnp.bfloat16),
            pltpu.VMEM((layers, rows, angles), jnp.bfloat16),
            pltpu.VMEM((rows, angles), jnp.bfloat16),
        ]
        + [pltpu.SemaphoreType.DMA((6,))]
        + [pltpu.SemaphoreType.DMA((count,))] * 4
        + [pltpu.SemaphoreType.DMA((layers,))] * 3
        + [pltpu.SemaphoreType.DMA((count,))] * 2,
        compiler_params=pltpu.CompilerParams(
            collective_id=0, has_side_effects=True, vmem_limit_bytes=WIDE_BYTES
        ),
        name="share",
    )(images, assign, rotation, group, table, rotations)

    residual, scores, average, lever = pl.pallas_call(
        compare_kernel,
        grid=(steps,),
        out_shape=(
            jax.ShapeDtypeStruct((number, rows, angles), jnp.bfloat16),
            jax.ShapeDtypeStruct((NROT, number), jnp.bfloat16),
            jax.ShapeDtypeStruct((rows, angles), jnp.bfloat16),
            jax.ShapeDtypeStruct((1, number), jnp.bfloat16),
        ),
        in_specs=[anywhere()] * 8 + [block],
        out_specs=(block, vmem(), vmem(), vmem()),
        scratch_shapes=[
            pltpu.SMEM((1, number), jnp.int32),
            pltpu.SMEM((1, number), jnp.int32),
            pltpu.VMEM((1, number), jnp.int32),
            pltpu.VMEM(table.shape, jnp.float32),
            pltpu.VMEM((count, rows, angles), jnp.bfloat16),
            pltpu.VMEM(rotations.shape, jnp.bfloat16),
            pltpu.SemaphoreType.DMA((8,)),
            pltpu.VMEM((shells, 128), jnp.float32),
        ]
        + [pltpu.VMEM((number * 8, angles), jnp.float32)] * 3,
        compiler_params=params,
        name="compare",
    )(assign, rotation, group, table, partner, average, lever, rotations, images)
    return (average[None, None], residual[None], scores.T[None], lever)


def solution(mesh):
    in_specs = (
        P("half", "cls", None, None),
        P("half", "cls"),
        P("half", "cls"),
        P("half", "cls"),
        P(),
    )
    out_specs = (
        P("half", "cls", None, None),
        P("half", "cls", None, None),
        P("half", "cls", None),
        P("half", "cls"),
    )
    return jax.shard_map(body, mesh=mesh, in_specs=in_specs, out_specs=out_specs, check_vma=False)
```

```python
import functools
import math

import jax
import jax.numpy as jnp
import numpy as np
from jax import lax
from jax.experimental import pallas as pl
from jax.experimental.pallas import tpu as pltpu
from jax.sharding import PartitionSpec as P

NROT = 36
TAU = 1.0
STEP = 32
BATCH = 4
QUAD = 4
MESH = pl.DeviceIdType.MESH
HIGHEST = lax.Precision.HIGHEST
WIDE_BYTES = 62 * 1024 * 1024


def vmem():
    return pl.BlockSpec(memory_space=pltpu.VMEM)


def anywhere():
    return pl.BlockSpec(memory_space=pl.ANY)


def mix(turn, angles):
    scaled = turn * angles
    offset = scaled // NROT
    fraction = (scaled - offset * NROT).astype(jnp.float32) / NROT
    first = (1.0 - fraction).astype(jnp.bfloat16).astype(jnp.float32)
    second = fraction.astype(jnp.bfloat16).astype(jnp.float32)
    return offset, first, second


def rotation_table(angles):
    turns = np.arange(NROT)
    offset = turns * angles // NROT
    fraction = (turns * angles % NROT).astype(np.float32) / np.float32(NROT)
    table = np.zeros((NROT, angles, angles), np.float32)
    source = np.arange(angles)
    for r in range(NROT):
        table[r, source, (source + offset[r]) % angles] = np.float32(1.0) - fraction[r]
        table[r, source, (source + offset[r] + 1) % angles] = fraction[r]
    return jnp.asarray(table.astype(jnp.bfloat16))


def align(image, rotation):
    return jnp.dot(image, rotation, preferred_element_type=jnp.float32)


def one_hot(row, size):
    places = lax.broadcasted_iota(jnp.int32, (size, row.shape[1]), 0)
    return (places == row).astype(jnp.float32)


def columns_of(ctf, groups):
    return lax.dot_general(
        ctf,
        one_hot(groups, ctf.shape[1]),
        (((1,), (0,)), ((), ())),
        precision=HIGHEST,
        preferred_element_type=jnp.float32,
    )


def fill_columns(columns_ref, ctf_ref, group_ref):
    columns_ref[...] = jnp.zeros_like(columns_ref)
    columns_ref[:, : group_ref.shape[1]] = columns_of(ctf_ref[...], group_ref[...])


def step_columns(columns_ref, step):
    lanes = columns_ref.shape[1]
    return pltpu.roll(columns_ref[...], lax.rem(lanes - step * STEP, lanes), 1)


def stacked(columns, place, lanes):
    column = columns[:, place : place + 1]
    wide = jnp.broadcast_to(column, (columns.shape[0], lanes))
    return jnp.concatenate([wide, wide], axis=0)


def share_kernel(
    count,
    cap,
    images_hbm,
    assign_hbm,
    turn_hbm,
    group_hbm,
    ctf_hbm,
    table_hbm,
    average_ref,
    lever_ref,
    partner_ref,
    images_ref,
    assign_ref,
    turn_ref,
    group_ref,
    ctf_ref,
    table_ref,
    order_row,
    order_ref,
    slot_weights,
    sums_ref,
    own_sums,
    own_code,
    codes,
    landed,
    staged,
    gathered,
    average,
    loads,
    code_send,
    code_recv,
    quad_send,
    quad_recv,
    far_send,
    far_recv,
    avg_send,
    pass_send,
    avg_recv,
):
    half = lax.axis_index("half")
    me = lax.axis_index("cls")
    other = 1 - half
    layers = count // QUAD
    layer = me // QUAD
    spot = me % QUAD
    particles = assign_ref.shape[1]
    slots = count * cap

    pairs = (
        (assign_hbm, assign_ref),
        (group_hbm, group_ref),
        (ctf_hbm, ctf_ref),
        (turn_hbm, turn_ref),
        (images_hbm, images_ref),
        (table_hbm, table_ref),
    )
    moves = [pltpu.make_async_copy(a, b, loads.at[n]) for n, (a, b) in enumerate(pairs)]
    for move in moves:
        move.start()

    barrier = pltpu.get_barrier_semaphore()

    def greet(k, _):
        peer = lax.rem(me + k, count)
        pl.semaphore_signal(barrier, inc=1, device_id=(half, peer), device_id_type=MESH)
        return 0

    def greet_other(k, _):
        peer = lax.rem(layer + k, layers) * QUAD + spot
        pl.semaphore_signal(barrier, inc=1, device_id=(other, peer), device_id_type=MESH)
        return 0

    lax.fori_loop(1, count, greet, 0)
    lax.fori_loop(0, layers, greet_other, 0)
    for move in moves[:3]:
        move.wait()
    own_code[0] = jnp.concatenate([assign_ref[...], group_ref[...]], axis=1).astype(jnp.float32)
    line = lax.broadcasted_iota(jnp.int32, (particles, particles), 0)
    across = lax.broadcasted_iota(jnp.int32, (particles, particles), 1)

    def as_column(row):
        return jnp.sum(jnp.where(line == across, row, 0), axis=1, keepdims=True)

    same = (as_column(assign_ref[...]) == assign_ref[...]) & (line < across)
    rank = jnp.sum(jnp.where(same, 1, 0), axis=0, keepdims=True)
    places = assign_ref[...] * cap + rank
    taken = one_hot(places, slots)
    filled = as_column(places) == lax.broadcasted_iota(jnp.int32, (particles, slots), 1)
    numbers = lax.broadcasted_iota(jnp.int32, (particles, slots), 0)
    order_row[...] = jnp.sum(jnp.where(filled, numbers, 0), axis=0, keepdims=True)

    def to_slots(values):
        return lax.dot_general(
            values,
            taken,
            (((1,), (1,)), ((), ())),
            precision=HIGHEST,
            preferred_element_type=jnp.float32,
        )

    order_move = pltpu.make_async_copy(order_row, order_ref, loads.at[0])
    order_move.start()
    weights = columns_of(ctf_ref[...], group_ref[...])
    slot_weights[...] = to_slots(weights)
    order_move.wait()
    for move in moves[3:]:
        move.wait()
    pl.semaphore_wait(barrier, count - 1 + layers)

    def code_copy(source, peer):
        return pltpu.make_async_remote_copy(
            src_ref=own_code.at[0],
            dst_ref=codes.at[source],
            send_sem=code_send.at[peer],
            recv_sem=code_recv.at[source],
            device_id=(half, peer),
            device_id_type=MESH,
        )

    def quad_copy(level, source, target):
        return pltpu.make_async_remote_copy(
            src_ref=sums_ref.at[level * QUAD + target],
            dst_ref=landed.at[level * QUAD + source],
            send_sem=quad_send.at[level * QUAD + target],
            recv_sem=quad_recv.at[level * QUAD + source],
            device_id=(half, layer * QUAD + target),
            device_id_type=MESH,
        )

    def far_copy(source, target):
        return pltpu.make_async_remote_copy(
            src_ref=staged.at[target],
            dst_ref=gathered.at[source],
            send_sem=far_send.at[target],
            recv_sem=far_recv.at[source],
            device_id=(half, target * QUAD + spot),
            device_id_type=MESH,
        )

    def avg_copy(source, target):
        return pltpu.make_async_remote_copy(
            src_ref=average,
            dst_ref=partner_ref.at[source * QUAD + spot],
            send_sem=avg_send.at[target],
            recv_sem=avg_recv.at[source * QUAD + spot],
            device_id=(other, target * QUAD + spot),
            device_id_type=MESH,
        )

    def pass_copy(level, source, target):
        return pltpu.make_async_remote_copy(
            src_ref=partner_ref.at[level * QUAD + source],
            dst_ref=partner_ref.at[level * QUAD + source],
            send_sem=pass_send.at[level * QUAD + target],
            recv_sem=avg_recv.at[level * QUAD + source],
            device_id=(half, layer * QUAD + target),
            device_id_type=MESH,
        )


    def class_sum(owner):
        columns = pltpu.roll(slot_weights[...], lax.rem(slots - owner * cap, slots), 1)
        total = jnp.zeros(images_ref.shape[1:], jnp.float32)
        for place in range(cap):
            particle = jnp.clip(order_ref[0, owner * cap + place], 0, images_ref.shape[0] - 1)
            image = align(images_ref[particle], table_ref[turn_ref[0, particle]])
            total += stacked(columns, place, image.shape[1]) * image
        return total

    def quad_sum(level):
        total = own_sums[level]
        for j in range(1, QUAD):
            source = lax.rem(spot + j, QUAD)
            quad_copy(level, source, source).wait_recv()
            total += landed[level * QUAD + source].astype(jnp.float32)
        return total

    def send_far(k, _):
        level = lax.rem(layer + k, layers)
        staged[level] = quad_sum(level).astype(jnp.bfloat16)
        far_copy(layer, level).start()
        return 0

    def sum_level(k, _):
        level = lax.rem(layer + k, layers)
        for pair in range(1, QUAD, 2):
            targets = [lax.rem(spot + j, QUAD) for j in (pair, pair + 1)]
            totals = [class_sum(level * QUAD + target) for target in targets]
            for j, target, total in zip((pair, pair + 1), targets, totals):
                if j < QUAD:
                    sums_ref[level * QUAD + target] = total.astype(jnp.bfloat16)
                    quad_copy(level, spot, target).start()
                else:
                    own_sums[level] = total

        for j in range(1, QUAD):
            code_copy(me, level * QUAD + lax.rem(spot + j, QUAD)).start()

        @pl.when(k < layers)
        def _():
            code_copy(me, level * QUAD + spot).start()

        @pl.when(k > 1)
        def _():
            send_far(k - 1, 0)

        return 0

    lax.fori_loop(1, layers + 1, sum_level, 0)

    def tally(code):
        owners = one_hot(code[:, :particles].astype(jnp.int32), count)
        kinds = one_hot(code[:, particles:].astype(jnp.int32), ctf_ref.shape[1])
        return lax.dot_general(
            owners.astype(jnp.bfloat16),
            kinds.astype(jnp.bfloat16),
            (((1,), (1,)), ((), ())),
            preferred_element_type=jnp.float32,
        )

    def add_code(k, counts):
        source = lax.rem(me + count - k, count)
        return counts + tally(codes[source])

    def wait_code(k, _):
        source = lax.rem(me + count - k, count)
        code_copy(source, source).wait_recv()
        return 0

    lax.fori_loop(1, count, wait_code, 0)
    counts = lax.fori_loop(1, count, add_code, tally(own_code[0]), unroll=min(count - 1, 15))
    table = ctf_ref[...]
    den = lax.dot_general(
        table * table,
        counts,
        (((1,), (1,)), ((), ())),
        precision=HIGHEST,
        preferred_element_type=jnp.float32,
    )
    mine = lax.broadcasted_iota(jnp.int32, den.shape, 1) == me
    column = jnp.sum(jnp.where(mine, den, 0.0), axis=1, keepdims=True) + TAU
    denom = jnp.concatenate([column, column], axis=0)

    def add_far(k, total):
        source = lax.rem(layer + count - k, layers)
        far_copy(source, source).wait_recv()
        return total + gathered[source].astype(jnp.float32)

    total = lax.fori_loop(1, layers, add_far, quad_sum(layer))
    average[...] = (total / denom).astype(jnp.bfloat16)

    def send_avg(k, _):
        avg_copy(layer, lax.rem(layer + k, layers)).start()
        return 0

    lax.fori_loop(0, layers, send_avg, 0)
    average_ref[...] = average[...]
    chosen = jnp.dot(
        den,
        one_hot(assign_ref[...], count),
        precision=HIGHEST,
        preferred_element_type=jnp.float32,
    )
    lever = jnp.sum(weights * weights / (chosen + TAU), axis=0, keepdims=True)
    lever_ref[...] = (lever / table.shape[0]).astype(jnp.bfloat16)

    def pass_on(k, _):
        level = lax.rem(layer + k, layers)
        avg_copy(level, level).wait_recv()
        for j in range(1, QUAD):
            pass_copy(level, spot, lax.rem(spot + j, QUAD)).start()
        return 0

    lax.fori_loop(0, layers, pass_on, 0)

    def finish_code(k, _):
        code_copy(me, lax.rem(me + k, count)).wait_send()
        return 0

    def finish_far(k, _):
        far_copy(layer, lax.rem(layer + k, layers)).wait_send()
        return 0

    def finish_level(k, _):
        level = lax.rem(layer + k, layers)
        avg_copy(layer, level).wait_send()
        for j in range(1, QUAD):
            peer = lax.rem(spot + j, QUAD)
            quad_copy(level, spot, peer).wait_send()
            pass_copy(level, peer, peer).wait_recv()
            pass_copy(level, spot, peer).wait_send()
        return 0

    lax.fori_loop(1, count, finish_code, 0)
    lax.fori_loop(1, layers, finish_far, 0)
    lax.fori_loop(0, layers, finish_level, 0)


def compare_kernel(
    assign_hbm,
    turn_hbm,
    group_hbm,
    ctf_hbm,
    partner_hbm,
    average_hbm,
    lever_hbm,
    table_hbm,
    images_ref,
    residual_ref,
    scores_ref,
    average_out,
    lever_out,
    assign_ref,
    turn_ref,
    group_ref,
    ctf_ref,
    partner_ref,
    table_ref,
    loads,
    columns_ref,
    image_power,
    predicted_power,
    folded,
):
    step = pl.program_id(0)

    @pl.when(step == 0)
    def _():
        pairs = (
            (group_hbm, group_ref),
            (ctf_hbm, ctf_ref),
            (assign_hbm, assign_ref),
            (turn_hbm, turn_ref),
            (average_hbm, average_out),
            (lever_hbm, lever_out),
            (partner_hbm, partner_ref),
            (table_hbm, table_ref),
        )
        moves = [pltpu.make_async_copy(a, b, loads.at[n]) for n, (a, b) in enumerate(pairs)]
        for move in moves:
            move.start()
        for move in moves[:2]:
            move.wait()
        fill_columns(columns_ref, ctf_ref, group_ref)
        for move in moves[2:]:
            move.wait()

    columns = step_columns(columns_ref, step)
    rows, angles = images_ref.shape[1:]

    def fold(values):
        return jnp.sum(values.reshape(rows // 8, 8, angles), axis=0)

    def work(place):
        particle = step * STEP + place
        raw_image = images_ref[place]
        image = raw_image.astype(jnp.float32)
        weight = stacked(columns, place, angles)
        owner = assign_ref[0, particle]
        rounded = (weight * partner_ref[owner].astype(jnp.float32)).astype(jnp.bfloat16)
        predicted = rounded.astype(jnp.float32)
        aligned = align(raw_image, table_ref[turn_ref[0, particle]])
        residual = (aligned - predicted).astype(jnp.bfloat16)
        cross = lax.dot_general(
            raw_image, rounded, (((0,), (0,)), ((), ())), preferred_element_type=jnp.float32
        )
        turned = cross[:8]
        for tile in range(1, angles // 8):
            turned += pltpu.roll(cross[tile * 8 : tile * 8 + 8], angles - tile * 8, 1)
        return residual, turned, fold(image * image), fold(predicted * predicted)

    for start in range(0, STEP, BATCH):
        places = range(start, start + BATCH)
        results = [work(place) for place in places]
        for place, (residual, turned, first, second) in zip(places, results):
            spot = pl.ds(pl.multiple_of((step * STEP + place) * 8, 8), 8)
            residual_ref[place] = residual
            folded[spot, :] = turned
            image_power[spot, :] = first
            predicted_power[spot, :] = second

    @pl.when(step == pl.num_programs(0) - 1)
    def _():
        number = folded.shape[0] // 8

        def part(ref, k):
            return ref[pl.ds(k, number, stride=8), :]

        corr = part(folded, 0)
        first = part(image_power, 0)
        second = part(predicted_power, 0)
        for k in range(1, 8):
            corr += pltpu.roll(part(folded, k), angles - k, 1)
            first += part(image_power, k)
            second += part(predicted_power, k)
        pixels = rows * angles
        ones = jnp.ones((1, angles), jnp.float32)

        def across(left, right, dims):
            return lax.dot_general(
                left, right, (dims, ((), ())), precision=HIGHEST, preferred_element_type=jnp.float32
            )

        first = jnp.sqrt(across(ones, first, ((1,), (1,))) / pixels + 1e-05)
        second = jnp.sqrt(across(ones, second, ((1,), (1,))) / pixels + 1e-05)
        turns = lax.broadcasted_iota(jnp.int32, (angles, angles), 1)
        shifts = lax.broadcasted_iota(jnp.int32, (angles, angles), 0)
        offset, one, two = mix(turns, angles)
        offset = lax.rem(offset, angles)
        table = jnp.where(shifts == offset, one, 0.0) + jnp.where(
            shifts == lax.rem(offset + 1, angles), two, 0.0
        )
        raw = across(table, corr, ((0,), (1,)))
        scores = raw / (math.sqrt(pixels) * first * second)
        scores_ref[...] = scores[:NROT].astype(jnp.bfloat16)


def body(particles, assign, rotation, group, ctf):
    images = particles[0]
    number, rows, angles = images.shape
    table = ctf.T
    rotations = rotation_table(angles)
    shells = ctf.shape[1]
    count = lax.axis_size("cls")
    layers = count // QUAD
    steps = number // STEP
    cap = max(2, 2 * number // count)
    slots = count * cap
    params = pltpu.CompilerParams(vmem_limit_bytes=WIDE_BYTES)
    block = pl.BlockSpec((STEP, rows, angles), lambda i: (i, 0, 0))

    average, lever, partner = pl.pallas_call(
        functools.partial(share_kernel, count, cap),
        out_shape=(
            jax.ShapeDtypeStruct((rows, angles), jnp.bfloat16),
            jax.ShapeDtypeStruct((1, number), jnp.bfloat16),
            jax.ShapeDtypeStruct((count, rows, angles), jnp.bfloat16),
        ),
        in_specs=[anywhere()] * 6,
        out_specs=(vmem(), vmem(), pl.BlockSpec(memory_space=pl.ANY)),
        scratch_shapes=[
            pltpu.VMEM((number, rows, angles), jnp.bfloat16),
            pltpu.VMEM((1, number), jnp.int32),
            pltpu.SMEM((1, number), jnp.int32),
            pltpu.VMEM((1, number), jnp.int32),
            pltpu.VMEM(table.shape, jnp.float32),
            pltpu.VMEM(rotations.shape, jnp.bfloat16),
            pltpu.VMEM((1, slots), jnp.int32),
            pltpu.SMEM((1, slots), jnp.int32),
            pltpu.VMEM((shells, slots), jnp.float32),
            pltpu.VMEM((count, rows, angles), jnp.bfloat16),
            pltpu.VMEM((layers, rows, angles), jnp.float32),
            pltpu.VMEM((1, 1, 2 * number), jnp.float32),
            pltpu.VMEM((count, 1, 2 * number), jnp.float32),
            pltpu.VMEM((count, rows, angles), jnp.bfloat16),
            pltpu.VMEM((layers, rows, angles), jnp.bfloat16),
            pltpu.VMEM((layers, rows, angles), jnp.bfloat16),
            pltpu.VMEM((rows, angles), jnp.bfloat16),
        ]
        + [pltpu.SemaphoreType.DMA((6,))]
        + [pltpu.SemaphoreType.DMA((count,))] * 4
        + [pltpu.SemaphoreType.DMA((layers,))] * 3
        + [pltpu.SemaphoreType.DMA((count,))] * 2,
        compiler_params=pltpu.CompilerParams(
            collective_id=0, has_side_effects=True, vmem_limit_bytes=WIDE_BYTES
        ),
        name="share",
    )(images, assign, rotation, group, table, rotations)

    residual, scores, average, lever = pl.pallas_call(
        compare_kernel,
        grid=(steps,),
        out_shape=(
            jax.ShapeDtypeStruct((number, rows, angles), jnp.bfloat16),
            jax.ShapeDtypeStruct((NROT, number), jnp.bfloat16),
            jax.ShapeDtypeStruct((rows, angles), jnp.bfloat16),
            jax.ShapeDtypeStruct((1, number), jnp.bfloat16),
        ),
        in_specs=[anywhere()] * 8 + [block],
        out_specs=(block, vmem(), vmem(), vmem()),
        scratch_shapes=[
            pltpu.SMEM((1, number), jnp.int32),
            pltpu.SMEM((1, number), jnp.int32),
            pltpu.VMEM((1, number), jnp.int32),
            pltpu.VMEM(table.shape, jnp.float32),
            pltpu.VMEM((count, rows, angles), jnp.bfloat16),
            pltpu.VMEM(rotations.shape, jnp.bfloat16),
            pltpu.SemaphoreType.DMA((8,)),
            pltpu.VMEM((shells, 128), jnp.float32),
        ]
        + [pltpu.VMEM((number * 8, angles), jnp.float32)] * 3,
        compiler_params=params,
        name="compare",
    )(assign, rotation, group, table, partner, average, lever, rotations, images)
    return (average[None, None], residual[None], scores.T[None], lever)


def solution(mesh):
    in_specs = (
        P("half", "cls", None, None),
        P("half", "cls"),
        P("half", "cls"),
        P("half", "cls"),
        P(),
    )
    out_specs = (
        P("half", "cls", None, None),
        P("half", "cls", None, None),
        P("half", "cls", None),
        P("half", "cls"),
    )
    return jax.shard_map(body, mesh=mesh, in_specs=in_specs, out_specs=out_specs, check_vma=False)
```
